32 devices in a mesh: seq: 16 (over z, x, core), head: 2 (over y).
Axes of the slice: x: 2, y: 2, z: 4, core: 2. Of those that a mesh axis runs over, the one named last changes fastest.
Arguments:
- queries: bfloat16 [4096, 5120], P('seq', 'head'), may hold values from -6 to 6
- keys_in: bfloat16 [4096, 5120], P('seq', 'head'), may hold values from -6 to 6
- values_in: bfloat16 [4096, 5120], P('seq', 'head'), may hold values from -162 to 162
- gain: bfloat16 [5120], P('head'), may hold values from 0.5 to 1.5
- upstream: bfloat16 [4096, 5120], P('seq', 'head'), may hold values from -6 to 6
Outputs:
- normed: bfloat16 [4096, 5120], P('seq', 'head')
- grad_queries: bfloat16 [4096, 5120], P('seq', 'head')
- grad_keys: bfloat16 [4096, 5120], P('seq', 'head')
- grad_values: bfloat16 [4096, 5120], P('seq', 'head')
The draws below stay inside these ranges and needn't reach their ends.
All inputs are finite; a program needn't handle non-finite values.
Results may differ from the reference program's by a relative error of at most 0.015.
Values may be sent and summed in bfloat16 or wider, within the bound.
A program may use at most 192 MiB of HBM per device.

```python
import math
import jax
import jax.numpy as jnp
from jax import lax

H = 40
HEAD_WIDTH = 128
BLK = 64
LEV = 5
TOKEN_COUNT = 4096


def draw_queries(key, part):
    draw_shape = (TOKEN_COUNT, H * HEAD_WIDTH)
    base_draw = jnp.clip(jax.random.normal(jax.random.fold_in(key, 1), draw_shape, jnp.float32), -6.0, 6.0)
    return base_draw.astype(jnp.bfloat16)


def draw_keys_in(key, part):
    draw_shape = (TOKEN_COUNT, H * HEAD_WIDTH)
    base_draw = jnp.clip(jax.random.normal(jax.random.fold_in(key, 2), draw_shape, jnp.float32), -6.0, 6.0)
    return base_draw.astype(jnp.bfloat16)


def draw_values_in(key, part):
    draw_shape = (TOKEN_COUNT, H * HEAD_WIDTH)
    base_draw = jnp.clip(jax.random.normal(jax.random.fold_in(key, 3), draw_shape, jnp.float32), -4.0, 4.0)
    head_ids = (jnp.arange(H * HEAD_WIDTH) // HEAD_WIDTH).astype(jnp.float32)
    jitter = jnp.exp(jax.random.uniform(jax.random.fold_in(key, 4), (H,), jnp.float32, 0.0, math.log(1.5)))
    head_scale = 3.0 ** (2.0 * head_ids / max(H - 1, 1)) * jnp.repeat(jitter, HEAD_WIDTH)
    row_scale = jnp.exp(jax.random.uniform(jax.random.fold_in(key, 5), (TOKEN_COUNT,), jnp.float32, 0.0, math.log(3.0)))
    return (base_draw * head_scale[None, :] * row_scale[:, None]).astype(jnp.bfloat16)


def block_scale(stream_key, shape, cuts, least, top_value):
    def one(dim, parts):
        steps = jax.random.uniform(jax.random.fold_in(jax.random.fold_in(stream_key, 6), dim), (parts,), jnp.float32, least / len(cuts), top_value / len(cuts))
        return jnp.repeat(jnp.exp(steps), shape[dim] // parts).reshape((-1,) + (1,) * (len(shape) - dim - 1))

    loudness = one(*cuts[0])
    for cut in cuts[1:]:
        loudness = loudness * one(*cut)
    return loudness


def scatter_about(own_key, shape, scale, most, split=(), kind=jnp.bfloat16):
    values = scale * jax.random.normal(own_key, shape, jnp.float32)
    if split:
        values = values * block_scale(own_key, shape, split, -0.22, 0.18)
    return jnp.clip(values, -most, most).astype(kind)


def setup_inputs(seed: int = 0) -> dict:
    key_of = jax.random.split(jax.random.key(seed), 6)
    queries = draw_queries(jax.random.fold_in(key_of[5], 71), 0)
    keys_in = draw_keys_in(jax.random.fold_in(key_of[5], 71), 0)
    values_in = draw_values_in(jax.random.fold_in(key_of[5], 71), 0)
    gain = jnp.clip(1.0 + 0.1 * jax.random.normal(key_of[3], (H * HEAD_WIDTH,), jnp.float32), 0.5, 1.5).astype(jnp.bfloat16)
    upstream = scatter_about(key_of[4], (TOKEN_COUNT, H * HEAD_WIDTH), 1.0, 6.0, ((0, 16), (1, 2)))
    return {"queries": queries, "keys_in": keys_in, "values_in": values_in, "gain": gain, "upstream": upstream}


LOG_TWO = 0.6931471805599453
EPSILON = 1e-06

def coarsen(rows_in):
    pairs = rows_in.reshape(rows_in.shape[0] // 2, 2, rows_in.shape[1])
    rounded = lax.optimization_barrier((0.5 * (pairs[:, 0] + pairs[:, 1])).astype(jnp.bfloat16))
    return rounded.astype(jnp.float32)

def key_set(head_q, head_k, head_v):
    count = TOKEN_COUNT // BLK
    query_matrix_rows = head_q.astype(jnp.float32).reshape(count, BLK, HEAD_WIDTH)
    key_sets = []
    for source in (head_k, head_v):
        full_rows = source.astype(jnp.float32)
        zeros_block = jnp.zeros((BLK, HEAD_WIDTH), jnp.float32)
        padded = jnp.concatenate([zeros_block, full_rows, zeros_block], 0)
        band_rows = jnp.stack([padded[offset * BLK:offset * BLK + TOKEN_COUNT].reshape(count, BLK, HEAD_WIDTH) for offset in range(3)], 1)
        pieces = [band_rows.reshape(count, 3 * BLK, HEAD_WIDTH)]
        level_rows = full_rows
        for level_num in range(1, LEV + 1):
            level_rows = coarsen(level_rows)
            supers = level_rows.reshape(count >> level_num, BLK, HEAD_WIDTH)
            sibling = supers.reshape(count >> level_num + 1, 2, BLK, HEAD_WIDTH)[:, ::-1].reshape(count >> level_num, BLK, HEAD_WIDTH)
            pieces.append(jnp.repeat(sibling, 2 ** level_num, axis=0))
        key_sets.append(jnp.concatenate(pieces, 1))
    return (query_matrix_rows, key_sets[0], key_sets[1])

def mask_bias():
    count = TOKEN_COUNT // BLK
    block_ids = jnp.arange(count)
    band_valid = jnp.stack([(block_ids + offset - 1 >= 0) & (block_ids + offset - 1 < count) for offset in range(3)], 1)
    valid_mask = jnp.concatenate([jnp.repeat(band_valid, BLK, axis=1), jnp.ones((count, LEV * BLK), bool)], 1)
    level_bias = jnp.concatenate([jnp.zeros((3 * BLK,), jnp.float32), jnp.repeat(LOG_TWO * jnp.arange(1, LEV + 1).astype(jnp.float32), BLK)])
    return (valid_mask, level_bias)

def head_probs(query_matrix_rows, key_matrix_rows):
    valid_mask, level_bias = mask_bias()
    unscaled_scores = jnp.einsum('tfz,tez->tfe', query_matrix_rows, key_matrix_rows, precision=lax.Precision.HIGHEST)
    scores = jnp.where(valid_mask[:, None, :], unscaled_scores * HEAD_WIDTH ** (-0.5) + level_bias, -jnp.inf)
    row_max = lax.optimization_barrier(jnp.max(scores, -1, keepdims=True))
    exp_terms = jnp.exp(scores - row_max)
    return exp_terms / lax.optimization_barrier(jnp.sum(exp_terms, -1, keepdims=True))

def head_forward(operands):
    query_matrix_rows, key_matrix_rows, value_matrix_rows = key_set(*operands)
    probs = head_probs(query_matrix_rows, key_matrix_rows)
    lower_probabilities = lax.optimization_barrier(probs.astype(jnp.bfloat16)).astype(jnp.float32)
    blended_output = jnp.einsum('hor,hrv->hov', lower_probabilities, value_matrix_rows, precision=lax.Precision.HIGHEST)
    return blended_output.reshape(TOKEN_COUNT, HEAD_WIDTH).astype(jnp.bfloat16)

def fold_back(grad_rows):
    count = TOKEN_COUNT // BLK
    band_part = grad_rows[:, :3 * BLK].reshape(count, 3, BLK, HEAD_WIDTH)
    padded = jnp.zeros((count + 2, BLK, HEAD_WIDTH), jnp.float32)
    for offset in range(3):
        padded = padded.at[offset:offset + count].add(band_part[:, offset])
    total_grad = padded[1:count + 1].reshape(TOKEN_COUNT, HEAD_WIDTH)
    carried = jnp.zeros((TOKEN_COUNT >> LEV, HEAD_WIDTH), jnp.float32)
    for level_num in range(LEV, 0, -1):
        level_part = grad_rows[:, (2 + level_num) * BLK:(3 + level_num) * BLK]
        summed = level_part.reshape(count >> level_num, 2 ** level_num, BLK, HEAD_WIDTH).sum(1)
        owned_grad = summed.reshape(count >> level_num + 1, 2, BLK, HEAD_WIDTH)[:, ::-1].reshape(TOKEN_COUNT >> level_num, HEAD_WIDTH)
        carried = 0.5 * jnp.repeat(carried + owned_grad, 2, axis=0)
    return total_grad + carried

def head_backward(operands):
    head_q, head_k, head_v, head_d = operands
    query_matrix_rows, key_matrix_rows, value_matrix_rows = key_set(head_q, head_k, head_v)
    probs = head_probs(query_matrix_rows, key_matrix_rows)
    lower_probabilities = lax.optimization_barrier(probs.astype(jnp.bfloat16)).astype(jnp.float32)
    count = TOKEN_COUNT // BLK
    block_gradients = head_d.astype(jnp.float32).reshape(count, BLK, HEAD_WIDTH)
    probability_gradient = jnp.einsum('tfz,tez->tfe', block_gradients, value_matrix_rows, precision=lax.Precision.HIGHEST)
    inner_sum = lax.optimization_barrier(jnp.sum(probs * probability_gradient, -1, keepdims=True))
    score_gradient = lax.optimization_barrier((probs * (probability_gradient - inner_sum) * HEAD_WIDTH ** (-0.5)).astype(jnp.bfloat16)).astype(jnp.float32)
    query_gradient = jnp.einsum('hor,hrv->hov', score_gradient, key_matrix_rows, precision=lax.Precision.HIGHEST).reshape(TOKEN_COUNT, HEAD_WIDTH).astype(jnp.bfloat16)
    key_summands = jnp.einsum('mul,muw->mlw', score_gradient, query_matrix_rows, precision=lax.Precision.HIGHEST)
    value_summands = jnp.einsum('mul,muw->mlw', lower_probabilities, block_gradients, precision=lax.Precision.HIGHEST)
    return (query_gradient, fold_back(key_summands).astype(jnp.bfloat16), fold_back(value_summands).astype(jnp.bfloat16))

def by_head(matrix):
    return matrix.reshape(TOKEN_COUNT, H, HEAD_WIDTH).transpose(1, 0, 2)

def from_heads(stacked):
    return stacked.transpose(1, 0, 2).reshape(TOKEN_COUNT, H * HEAD_WIDTH)

def reference(queries, keys_in, values_in, gain, upstream):
    q_heads, k_heads, v_heads = (by_head(queries), by_head(keys_in), by_head(values_in))
    attended = from_heads(lax.map(head_forward, (q_heads, k_heads, v_heads)))
    attended_wide = attended.astype(jnp.float32)
    gain_wide = gain.astype(jnp.float32)
    columns = H * HEAD_WIDTH
    inv_rms = lax.rsqrt(lax.optimization_barrier(jnp.sum(attended_wide * attended_wide, -1, keepdims=True)) / columns + EPSILON)
    normed = (attended_wide * inv_rms * gain_wide).astype(jnp.bfloat16)
    scaled_grad = upstream.astype(jnp.float32) * gain_wide
    projection = lax.optimization_barrier(jnp.sum(scaled_grad * attended_wide, -1, keepdims=True))
    d_attended = (inv_rms * scaled_grad - attended_wide * (inv_rms * inv_rms * inv_rms) * projection / columns).astype(jnp.bfloat16)
    query_gradient, grad_k, grad_v = lax.map(head_backward, (q_heads, k_heads, v_heads, by_head(d_attended)))
    return (normed, from_heads(query_gradient), from_heads(grad_k), from_heads(grad_v))
```

```python
import functools
import jax
import jax.numpy as jnp
from jax import lax
from jax.experimental import pallas as pl
from jax.experimental.pallas import tpu as pltpu
from jax.sharding import PartitionSpec as P

HEAD_WIDTH = 128
BLK = 64
LEV = 5
EPSILON = 1e-06
LOG2E = 1.4426950408889634
MESH = pl.DeviceIdType.MESH
HEADS_STEP = 4
FAR = tuple(1 << k for k in range(LEV - 1))
F32, BF16 = jnp.float32, jnp.bfloat16
NN = (((1,), (0,)), ((), ()))
NT = (((1,), (1,)), ((), ()))
TN = (((0,), (0,)), ((), ()))


def dot(a, b, dims):
    return lax.dot_general(a, b, dims, preferred_element_type=F32)


def piece_shapes(cols):
    return [(n, 2 * BLK // n, cols) for n in FAR]


def exchange(me, count, far_src, far_dst, edge_src, edge_dst, sems, prepare):
    send_far, recv_far, send_edge, recv_edge = sems
    barrier = pltpu.get_barrier_semaphore()
    peers = []
    for k, n in enumerate(FAR):
        g, o = me // n, me % n
        base = (g + 1 - 2 * (g % 2)) * n
        for r in range(n):
            peers.append((k, n, r, base + (o + r) % n, (o + r) % n, o))
    has = (me > 0, me < count - 1)
    ids = (me - 1, me + 1)
    for peer in peers:
        pl.semaphore_signal(barrier, inc=1, device_id={"seq": peer[3]}, device_id_type=MESH)
    for side in range(2):
        @pl.when(has[side])
        def _():
            pl.semaphore_signal(barrier, inc=1, device_id={"seq": ids[side]}, device_id_type=MESH)
    pl.semaphore_wait(
        barrier, len(peers) + has[0].astype(jnp.int32) + has[1].astype(jnp.int32))

    def edge_copy(side, part):
        return pltpu.make_async_remote_copy(
            src_ref=edge_src(side, part), dst_ref=edge_dst(1 - side, part),
            send_sem=send_edge.at[side, part], recv_sem=recv_edge.at[1 - side, part],
            device_id={"seq": ids[side]}, device_id_type=MESH)

    def edge_wait(side, part):
        return pltpu.make_async_remote_copy(
            src_ref=edge_src(side, part), dst_ref=edge_dst(side, part),
            send_sem=send_edge.at[side, part], recv_sem=recv_edge.at[side, part],
            device_id={"seq": ids[side]}, device_id_type=MESH)

    for side in range(2):
        @pl.when(has[side])
        def _():
            for part in range(2):
                edge_copy(side, part).start()
    prepare()
    copies = []
    for k, n, r, dest, t, o in reversed(peers):
        copies.append(pltpu.make_async_remote_copy(
            src_ref=far_src(k, t), dst_ref=far_dst(k, o),
            send_sem=send_far.at[n - 1 + r], recv_sem=recv_far.at[n - 1 + r],
            device_id={"seq": dest}, device_id_type=MESH))
        copies[-1].start()
    for copy in copies:
        copy.wait()
    for side in range(2):
        @pl.when(has[side])
        def _():
            for part in range(2):
                edge_wait(side, part).wait_send()
                edge_wait(side, part).wait_recv()


def sem_shapes():
    total = sum(FAR)
    return [pltpu.SemaphoreType.DMA((total,)), pltpu.SemaphoreType.DMA((total,)),
            pltpu.SemaphoreType.DMA((2, 2)), pltpu.SemaphoreType.DMA((2, 2))]


def halve(x):
    n = x.shape[0]
    row = lax.broadcasted_iota(jnp.int32, (n // 2, n), 0)
    col = lax.broadcasted_iota(jnp.int32, (n // 2, n), 1)
    mat = jnp.where((col == 2 * row) | (col == 2 * row + 1), 0.5, 0.0).astype(BF16)
    return dot(mat, x, NN)


def gather_kernel(count, k_ref, v_ref, l1_ref, r2, r3, r4, r5, edge_ref,
                  s2, s3, s4, s5, *sems):
    me = lax.axis_index("seq")
    rows, cols = k_ref.shape
    far_scr, far_out = (s2, s3, s4, s5), (r2, r3, r4, r5)
    width = 4 * HEAD_WIDTH

    def prepare():
        def step(i, _):
            c = pl.ds(pl.multiple_of(i * width, width), width)
            for part, ref in enumerate((k_ref, v_ref)):
                level = halve(ref[:, c]).astype(BF16)
                l1_ref[part, :, c] = level
                for scr, n in zip((s2, s3, s4), FAR):
                    level = halve(level).astype(BF16)
                    m = BLK // n
                    scr[part * m:(part + 1) * m, c] = level
            last = jnp.concatenate(
                [halve(s4[:16, c]), halve(s4[16:, c])], 0)
            s5[:, c] = last.astype(BF16)
            return 0
        lax.fori_loop(0, cols // width, step, 0)

    def edge_src(side, part):
        ref = (k_ref, v_ref)[part]
        return ref.at[pl.ds(0, BLK)] if side == 0 else ref.at[pl.ds(rows - BLK, BLK)]

    exchange(me, count, lambda k, t: far_scr[k], lambda k, o: far_out[k].at[o],
             edge_src, lambda side, part: edge_ref.at[side, part], sems, prepare)


def send_kernel(count, g2, g3, g4, g5, eg, r2, r3, r4, r5, er, *sems):
    me = lax.axis_index("seq")
    src, dst = (g2, g3, g4, g5), (r2, r3, r4, r5)
    exchange(me, count, lambda k, t: src[k].at[t], lambda k, o: dst[k].at[o],
             lambda side, part: eg.at[side, part], lambda side, part: er.at[side, part],
             sems, lambda: None)


def keep(x, flag):
    return jnp.where(flag, x.astype(F32), 0.0).astype(BF16)


def load_sets(me, count, c, k_ref, v_ref, l1_ref, far_refs, edge_ref):
    sets = []
    for part, ref in enumerate((k_ref, v_ref)):
        x = ref[:, c]
        low = keep(edge_ref[0, part, :, c], me > 0)
        high = keep(edge_ref[1, part, :, c], me < count - 1)
        far = []
        for n, far_ref in zip(FAR, far_refs):
            m = BLK // n
            if m >= 16:
                far.append(far_ref[:, part * m:(part + 1) * m, c].reshape(BLK, HEAD_WIDTH))
            else:
                wide = far_ref[:, :, c].astype(F32)
                far.append(wide[:, part * m:(part + 1) * m].reshape(BLK, HEAD_WIDTH).astype(BF16))
        sets.append((
            jnp.concatenate([low, x[:3 * BLK], l1_ref[part, BLK:, c]] + far, 0),
            jnp.concatenate([x[BLK:], high, l1_ref[part, :BLK, c]] + far, 0)))
    return sets


def forward_kernel(count, q_ref, k_ref, v_ref, u_ref, gain_ref, bias_ref, l1_ref,
                   r2, r3, r4, r5, edge_ref, att_ref, lse_ref, stat_ref):
    me = lax.axis_index("seq")

    @pl.when(pl.program_id(0) == 0)
    def _():
        stat_ref[...] = jnp.zeros_like(stat_ref)

    for h in range(HEADS_STEP):
        c = slice(h * HEAD_WIDTH, (h + 1) * HEAD_WIDTH)
        keys, values = load_sets(me, count, c, k_ref, v_ref, l1_ref, (r2, r3, r4, r5), edge_ref)
        gain = gain_ref[:, c].astype(F32)
        for p in range(2):
            rows = slice(p * 2 * BLK, (p + 1) * 2 * BLK)
            s = dot(keys[p], q_ref[rows, c], NT) * (LOG2E * HEAD_WIDTH ** -0.5) + bias_ref[p]
            top = jnp.max(s, 0, keepdims=True)
            e = jnp.exp2(s - top)
            total = jnp.sum(e, 0, keepdims=True)
            low = (e * (1.0 / total)).astype(BF16)
            lse_ref[h, :, rows] = top + jnp.log2(total)
            att = dot(low, values[p], TN).astype(BF16)
            att_ref[rows, c] = att
            wide = att.astype(F32)
            sg = u_ref[rows, c].astype(F32) * gain
            stat_ref[0, rows, :] += wide * wide
            stat_ref[1, rows, :] += sg * wide


def backward_kernel(count, q_ref, k_ref, v_ref, u_ref, gain_ref, bias_ref, l1_ref,
                    r2, r3, r4, r5, edge_ref, att_ref, lse_ref, coef_ref,
                    norm_ref, gq_ref, loc_ref, gl1_ref, g2, g3, g4, g5, eg_ref):
    me = lax.axis_index("seq")
    scale = HEAD_WIDTH ** -0.5
    for h in range(HEADS_STEP):
        c = slice(h * HEAD_WIDTH, (h + 1) * HEAD_WIDTH)
        keys, values = load_sets(me, count, c, k_ref, v_ref, l1_ref, (r2, r3, r4, r5), edge_ref)
        gain = gain_ref[:, c].astype(F32)
        terms = []
        for p in range(2):
            rows = slice(p * 2 * BLK, (p + 1) * 2 * BLK)
            q = q_ref[rows, c]
            inv, back = coef_ref[rows, 0:1], coef_ref[rows, 1:2]
            wide = att_ref[rows, c].astype(F32)
            sg = u_ref[rows, c].astype(F32) * gain
            norm_ref[rows, c] = (wide * inv * gain).astype(BF16)
            d = (inv * sg - wide * back).astype(BF16)
            s = dot(keys[p], q, NT) * (LOG2E * scale) + bias_ref[p]
            probs = jnp.exp2(s - lse_ref[h, :, rows])
            dp = dot(values[p], d, NT)
            inner = jnp.sum(probs * dp, 0, keepdims=True)
            ds = (probs * (dp - inner) * scale).astype(BF16)
            gq_ref[rows, c] = dot(ds, keys[p], TN).astype(BF16)
            terms.append((dot(ds, q, NN), dot(probs.astype(BF16), d, NN)))
        for part in range(2):
            a, b = terms[0][part], terms[1][part]
            eg_ref[0, part, :, c] = a[:BLK].astype(BF16)
            eg_ref[1, part, :, c] = b[3 * BLK:4 * BLK].astype(BF16)
            loc_ref[part, :, c] = jnp.concatenate(
                [a[BLK:2 * BLK], a[2 * BLK:4 * BLK] + b[:2 * BLK], b[2 * BLK:3 * BLK]], 0)
            gl1_ref[part, :, c] = jnp.concatenate(
                [b[4 * BLK:5 * BLK], a[4 * BLK:5 * BLK]], 0).astype(BF16)
        both = [terms[0][part][5 * BLK:] + terms[1][part][5 * BLK:] for part in range(2)]
        for k, (n, g) in enumerate(zip(FAR, (g2, g3, g4, g5))):
            m = BLK // n
            parts = [x[k * BLK:(k + 1) * BLK].reshape(n, m, HEAD_WIDTH) for x in both]
            g[:, :, c] = jnp.concatenate(parts, 1).astype(BF16)


def combine_kernel(count, loc_ref, gl1_ref, r2, r3, r4, r5, er_ref, gk_ref, gv_ref):
    me = lax.axis_index("seq")
    row_count, span = gk_ref.shape
    flags = (me > 0, me < count - 1)
    row = lax.broadcasted_iota(jnp.int32, (row_count, 2 * BLK + 4 * BLK), 0)
    col = lax.broadcasted_iota(jnp.int32, (row_count, 2 * BLK + 4 * BLK), 1)
    mat = jnp.where((col < 2 * BLK) & (row // 2 == col), 0.5, 0.0)
    for k, n in enumerate(FAR):
        first = (2 + k) * BLK
        m = BLK // n
        inside = (col >= first) & (col < first + BLK)
        mat += jnp.where(inside & (row // (4 * n) == (col - first) % m), 0.25 / n, 0.0)
    mat = mat.astype(BF16)
    for part, out in enumerate((gk_ref, gv_ref)):
        far = [gl1_ref[part]]
        for n, ref in zip(FAR, (r2, r3, r4, r5)):
            m = BLK // n
            if m >= 16:
                far.append(ref[:, part * m:(part + 1) * m, :].reshape(BLK, span))
            else:
                wide = ref[...].astype(F32)
                far.append(wide[:, part * m:(part + 1) * m].reshape(BLK, span).astype(BF16))
        total = loc_ref[part] + dot(mat, jnp.concatenate(far, 0), NN)
        low = jnp.where(flags[0], er_ref[0, part].astype(F32), 0.0)
        high = jnp.where(flags[1], er_ref[1, part].astype(F32), 0.0)
        out[:BLK] = (total[:BLK] + low).astype(BF16)
        out[BLK:row_count - BLK] = total[BLK:row_count - BLK].astype(BF16)
        out[row_count - BLK:] = (total[row_count - BLK:] + high).astype(BF16)


def score_bias(seq_index, seq_count):
    key = jnp.arange(4 * BLK)[None, :, None] // BLK
    query = jnp.arange(2 * BLK)[None, None, :] // BLK
    pair = jnp.arange(2)[:, None, None]
    block = seq_index * 4 + 2 * pair + key - 1
    valid = (key >= query) & (key <= query + 2) & (block >= 0) & (block < 4 * seq_count)
    band = jnp.where(valid, 0.0, -1e30).astype(F32)
    levels = jnp.repeat(jnp.arange(1, LEV + 1).astype(F32), BLK)[None, :, None]
    return jnp.concatenate([band, jnp.broadcast_to(levels, (2, LEV * BLK, 2 * BLK))], 1)


def body(queries, keys_in, values_in, gain, upstream):
    rows, cols = queries.shape
    heads = cols // HEAD_WIDTH
    me = lax.axis_index("seq")
    count = lax.axis_size("seq")
    shape = jax.ShapeDtypeStruct
    any_spec = pl.BlockSpec(memory_space=pl.ANY)
    vmem = pl.BlockSpec(memory_space=pltpu.VMEM)
    pieces = piece_shapes(cols)
    piece_out = [shape(s, BF16) for s in pieces]
    edge_out = shape((2, 2, BLK, cols), BF16)
    limit = 48 * 1024 * 1024

    l1, *recv = pl.pallas_call(
        functools.partial(gather_kernel, count),
        out_shape=[shape((2, rows // 2, cols), BF16)] + piece_out + [edge_out],
        in_specs=[vmem] * 2,
        out_specs=[vmem] + [any_spec] * 5,
        scratch_shapes=[pltpu.VMEM(s[1:], BF16) for s in pieces] + sem_shapes(),
        compiler_params=pltpu.CompilerParams(
            collective_id=0, has_side_effects=True, vmem_limit_bytes=limit),
        name="gather_tiles",
    )(keys_in, values_in)
    bias = score_bias(me, count)
    gain2 = gain.reshape(1, cols)

    step = HEADS_STEP * HEAD_WIDTH
    grid = (heads // HEADS_STEP,)
    flat = lambda n: pl.BlockSpec((n, step), lambda i: (0, i))
    cube = lambda a, b: pl.BlockSpec((a, b, step), lambda i: (0, 0, i))
    quad = pl.BlockSpec((2, 2, BLK, step), lambda i: (0, 0, 0, i))
    fixed = lambda s: pl.BlockSpec(s, lambda i: (0,) * len(s))
    piece_specs = [cube(s[0], s[1]) for s in pieces]
    lse_spec = pl.BlockSpec((HEADS_STEP, 1, rows), lambda i: (i, 0, 0))
    shared = [flat(rows)] * 4 + [flat(1), fixed(bias.shape), cube(2, rows // 2)] + piece_specs + [quad]
    params = pltpu.CompilerParams(vmem_limit_bytes=limit)
    common = (queries, keys_in, values_in, upstream, gain2, bias, l1, *recv)
    att, lse, stat = pl.pallas_call(
        functools.partial(forward_kernel, count),
        grid=grid,
        out_shape=[shape((rows, cols), BF16), shape((heads, 1, rows), F32),
                   shape((2, rows, HEAD_WIDTH), F32)],
        in_specs=shared,
        out_specs=[flat(rows), lse_spec, fixed((2, rows, HEAD_WIDTH))],
        compiler_params=params,
        name="attend",
    )(*common)

    sums = jnp.sum(stat, -1)
    parts = lax.axis_size("head")
    total = sums
    for shift in range(1, parts):
        total = total + lax.ppermute(
            sums, "head", [(i, (i + shift) % parts) for i in range(parts)])
    columns = cols * parts
    inv = lax.rsqrt(total[0] / columns + EPSILON)
    coef = jnp.stack([inv, inv * inv * inv * total[1] / columns], 1)

    normed, gq, loc, gl1, *grads = pl.pallas_call(
        functools.partial(backward_kernel, count),
        grid=grid,
        out_shape=[shape((rows, cols), BF16)] * 2
        + [shape((2, rows, cols), F32), shape((2, rows // 2, cols), BF16)]
        + piece_out + [edge_out],
        in_specs=shared + [flat(rows), lse_spec, fixed((rows, 2))],
        out_specs=[flat(rows)] * 2 + [cube(2, rows), cube(2, rows // 2)] + piece_specs + [quad],
        compiler_params=params,
        name="differentiate",
    )(*common, att, lse, coef)

    back = pl.pallas_call(
        functools.partial(send_kernel, count),
        out_shape=piece_out + [edge_out],
        in_specs=[any_spec] * 5,
        out_specs=[any_spec] * 5,
        scratch_shapes=sem_shapes(),
        compiler_params=pltpu.CompilerParams(
            collective_id=1, has_side_effects=True, vmem_limit_bytes=limit),
        name="send_terms",
    )(*grads)

    gk, gv = pl.pallas_call(
        functools.partial(combine_kernel, count),
        grid=grid,
        out_shape=[shape((rows, cols), BF16)] * 2,
        in_specs=[cube(2, rows), cube(2, rows // 2)] + piece_specs + [quad],
        out_specs=[flat(rows)] * 2,
        compiler_params=params,
        name="combine",
    )(loc, gl1, *back)
    return normed, gq, gk, gv


def solution(mesh):
    spec = P("seq", "head")
    return jax.shard_map(
        body,
        mesh=mesh,
        in_specs=(spec, spec, spec, P("head"), spec),
        out_specs=(spec,) * 4,
        check_vma=False,
    )
```

```python
import functools
import jax
import jax.numpy as jnp
from jax import lax
from jax.experimental import pallas as pl
from jax.experimental.pallas import tpu as pltpu
from jax.sharding import PartitionSpec as P

HEAD_WIDTH = 128
BLK = 64
LEV = 5
EPSILON = 1e-06
LOG2E = 1.4426950408889634
MESH = pl.DeviceIdType.MESH
HEADS_STEP = 4
FAR = tuple(1 << k for k in range(LEV - 1))
F32, BF16 = jnp.float32, jnp.bfloat16
NN = (((1,), (0,)), ((), ()))
NT = (((1,), (1,)), ((), ()))
TN = (((0,), (0,)), ((), ()))


def dot(a, b, dims):
    return lax.dot_general(a, b, dims, preferred_element_type=F32)


def piece_shapes(cols):
    return [(n, 2 * BLK // n, cols) for n in FAR]


def exchange(me, count, edge_src, edge_dst, sems, run_far):
    send_edge, recv_edge = sems
    barrier = pltpu.get_barrier_semaphore()
    peers = []
    for k, n in enumerate(FAR):
        g, o = me // n, me % n
        base = (g + 1 - 2 * (g % 2)) * n
        for r in range(n):
            peers.append((k, n, r, base + (o + r) % n, (o + r) % n, o))
    has = (me > 0, me < count - 1)
    ids = (me - 1, me + 1)
    for peer in peers:
        pl.semaphore_signal(barrier, inc=1, device_id={"seq": peer[3]}, device_id_type=MESH)
    for side in range(2):
        @pl.when(has[side])
        def _():
            pl.semaphore_signal(barrier, inc=1, device_id={"seq": ids[side]}, device_id_type=MESH)
    pl.semaphore_wait(
        barrier, len(peers) + has[0].astype(jnp.int32) + has[1].astype(jnp.int32))

    def edge_copy(side, part):
        return pltpu.make_async_remote_copy(
            src_ref=edge_src(side, part), dst_ref=edge_dst(1 - side, part),
            send_sem=send_edge.at[side, part], recv_sem=recv_edge.at[1 - side, part],
            device_id={"seq": ids[side]}, device_id_type=MESH)

    def edge_wait(side, part):
        return pltpu.make_async_remote_copy(
            src_ref=edge_src(side, part), dst_ref=edge_dst(side, part),
            send_sem=send_edge.at[side, part], recv_sem=recv_edge.at[side, part],
            device_id={"seq": ids[side]}, device_id_type=MESH)

    for side in range(2):
        @pl.when(has[side])
        def _():
            for part in range(2):
                edge_copy(side, part).start()
    run_far(peers)
    for side in range(2):
        @pl.when(has[side])
        def _():
            for part in range(2):
                edge_wait(side, part).wait_send()
                edge_wait(side, part).wait_recv()


def remote(src, dst, sems, index, device):
    return pltpu.make_async_remote_copy(
        src_ref=src, dst_ref=dst, send_sem=sems[0].at[index], recv_sem=sems[1].at[index],
        device_id={"seq": device}, device_id_type=MESH)


def columns_of(core, half):
    return pl.ds(pl.multiple_of(core * half, HEAD_WIDTH), half)


def sem_shapes():
    total = sum(FAR)
    return [pltpu.SemaphoreType.DMA((total,))] * 4 + [
            pltpu.SemaphoreType.DMA((2, 2)), pltpu.SemaphoreType.DMA((2, 2))]


def halve(x):
    n = x.shape[0]
    row = lax.broadcasted_iota(jnp.int32, (n // 2, n), 0)
    col = lax.broadcasted_iota(jnp.int32, (n // 2, n), 1)
    mat = jnp.where((col == 2 * row) | (col == 2 * row + 1), 0.5, 0.0).astype(BF16)
    return dot(mat, x, NN)


def gather_kernel(count, k_ref, v_ref, l1_ref, r2, r3, r4, r5, edge_ref,
                  s2, s3, s4, s5, *sems):
    me = lax.axis_index("seq")
    rows, cols = k_ref.shape
    far_scr, far_out = (s2, s3, s4, s5), (r2, r3, r4, r5)
    width = 4 * HEAD_WIDTH

    def prepare():
        def step(i, _):
            c = pl.ds(pl.multiple_of(i * width, width), width)
            for part, ref in enumerate((k_ref, v_ref)):
                level = halve(ref[:, c]).astype(BF16)
                l1_ref[part, :, c] = level
                for scr, n in zip((s2, s3, s4), FAR):
                    level = halve(level).astype(BF16)
                    m = BLK // n
                    scr[part * m:(part + 1) * m, c] = level
            last = jnp.concatenate(
                [halve(s4[:16, c]), halve(s4[16:, c])], 0)
            s5[:, c] = last.astype(BF16)
            return 0
        lax.fori_loop(0, cols // width, step, 0)

    def edge_src(side, part):
        ref = (k_ref, v_ref)[part]
        return ref.at[pl.ds(0, BLK)] if side == 0 else ref.at[pl.ds(rows - BLK, BLK)]

    half = cols // 2
    core = me % 2
    mine = columns_of(core, half)

    def run_far(peers):
        prepare()
        order = peers[::-1]
        copies = []
        for k, n, r, dest, t, o in order:
            src, dst = far_scr[k], far_out[k].at[o]
            if n > 1:
                part = columns_of(t % 2, half)
                src, dst = src.at[:, part], dst.at[:, part]
            copies.append(remote(src, dst, sems[:2], n - 1 + r, dest))
            copies[-1].start()
        swaps = []
        for copy, (k, n, r, dest, t, o) in zip(copies, order):
            if n > 1:
                slot = far_out[k].at[(o + n - r) % n, :, mine]
                pltpu.make_async_remote_copy(
                    src_ref=slot, dst_ref=slot, send_sem=sems[0].at[n - 1 + r],
                    recv_sem=sems[1].at[n - 1 + r],
                    device_id={"seq": dest}, device_id_type=MESH).wait_recv()
                swaps.append(remote(slot, slot, sems[2:4], n - 1 + r, me + 1 - 2 * core))
                swaps[-1].start()
                copy.wait_send()
            else:
                copy.wait()
        for k, n, r, dest, t, o in order:
            if n > 1:
                theirs = (me + 1 - 2 * core) % n
                slot = far_out[k].at[(theirs + n - r) % n, :, columns_of(1 - core, half)]
                remote(slot, slot, sems[2:4], n - 1 + r, me + 1 - 2 * core).wait_recv()
        for swap in swaps:
            swap.wait_send()

    exchange(me, count, edge_src, lambda side, part: edge_ref.at[side, part], sems[4:], run_far)


def send_kernel(count, g2, g3, g4, g5, eg, r2, r3, r4, r5, er,
                a3, a4, a5, b3, b4, b5, load_sem, *sems):
    me = lax.axis_index("seq")
    src, dst = (g2, g3, g4, g5), (r2, r3, r4, r5)
    own, came = (None, a3, a4, a5), (None, b3, b4, b5)
    half = g2.shape[-1] // 2
    core = me % 2
    mate = me + 1 - 2 * core
    mine = columns_of(core, half)

    def run_far(peers):
        loads, swaps, copies = {}, {}, []
        for k in (3, 2, 1):
            swaps[k] = remote(src[k].at[:, :, columns_of(1 - core, half)], came[k],
                              sems[2:4], k, mate)
            swaps[k].start()
            loads[k] = pltpu.make_async_copy(src[k].at[:, :, mine], own[k], load_sem.at[k])
            loads[k].start()
        for level in (3, 2, 1, 0):
            if level:
                loads[level].wait()
                swaps[level].wait()

                def add(i, _, a=own[level], b=came[level]):
                    a[i] = (a[i].astype(F32) + b[i].astype(F32)).astype(BF16)
                    return 0
                lax.fori_loop(0, FAR[level], add, 0)
            for k, n, r, dest, t, o in peers:
                if k == level:
                    if k:
                        copy = remote(own[k].at[t], dst[k].at[o // 2, :, mine],
                                      sems[:2], n - 1 + r, dest)
                    else:
                        copy = remote(src[k].at[t], dst[k].at[o], sems[:2], n - 1 + r, dest)
                    copies.append(copy)
                    copy.start()
        for copy in copies:
            copy.wait()

    exchange(me, count, lambda side, part: eg.at[side, part],
             lambda side, part: er.at[side, part], sems[4:], run_far)


def keep(x, flag):
    return jnp.where(flag, x.astype(F32), 0.0).astype(BF16)


def load_sets(me, count, c, k_ref, v_ref, l1_ref, far_refs, edge_ref):
    sets = []
    for part, ref in enumerate((k_ref, v_ref)):
        x = ref[:, c]
        low = keep(edge_ref[0, part, :, c], me > 0)
        high = keep(edge_ref[1, part, :, c], me < count - 1)
        far = []
        for n, far_ref in zip(FAR, far_refs):
            m = BLK // n
            if m >= 16:
                far.append(far_ref[:, part * m:(part + 1) * m, c].reshape(BLK, HEAD_WIDTH))
            else:
                wide = far_ref[:, :, c].astype(F32)
                far.append(wide[:, part * m:(part + 1) * m].reshape(BLK, HEAD_WIDTH).astype(BF16))
        sets.append((
            jnp.concatenate([low, x[:3 * BLK], l1_ref[part, BLK:, c]] + far, 0),
            jnp.concatenate([x[BLK:], high, l1_ref[part, :BLK, c]] + far, 0)))
    return sets


def forward_kernel(count, q_ref, k_ref, v_ref, u_ref, gain_ref, bias_ref, l1_ref,
                   r2, r3, r4, r5, edge_ref, att_ref, lse_ref, stat_ref):
    me = lax.axis_index("seq")

    @pl.when(pl.program_id(0) == 0)
    def _():
        stat_ref[...] = jnp.zeros_like(stat_ref)

    for h in range(HEADS_STEP):
        c = slice(h * HEAD_WIDTH, (h + 1) * HEAD_WIDTH)
        keys, values = load_sets(me, count, c, k_ref, v_ref, l1_ref, (r2, r3, r4, r5), edge_ref)
        gain = gain_ref[:, c].astype(F32)
        for p in range(2):
            rows = slice(p * 2 * BLK, (p + 1) * 2 * BLK)
            s = dot(keys[p], q_ref[rows, c], NT) * (LOG2E * HEAD_WIDTH ** -0.5) + bias_ref[p]
            top = jnp.max(s, 0, keepdims=True)
            e = jnp.exp2(s - top)
            total = jnp.sum(e, 0, keepdims=True)
            low = (e * (1.0 / total)).astype(BF16)
            lse_ref[h, :, rows] = top + jnp.log2(total)
            att = dot(low, values[p], TN).astype(BF16)
            att_ref[rows, c] = att
            wide = att.astype(F32)
            sg = u_ref[rows, c].astype(F32) * gain
            stat_ref[0, rows, :] += wide * wide
            stat_ref[1, rows, :] += sg * wide


def backward_kernel(count, q_ref, k_ref, v_ref, u_ref, gain_ref, bias_ref, l1_ref,
                    r2, r3, r4, r5, edge_ref, att_ref, lse_ref, coef_ref,
                    norm_ref, gq_ref, loc_ref, gl1_ref, g2, g3, g4, g5, eg_ref):
    me = lax.axis_index("seq")
    scale = HEAD_WIDTH ** -0.5
    for h in range(HEADS_STEP):
        c = slice(h * HEAD_WIDTH, (h + 1) * HEAD_WIDTH)
        keys, values = load_sets(me, count, c, k_ref, v_ref, l1_ref, (r2, r3, r4, r5), edge_ref)
        gain = gain_ref[:, c].astype(F32)
        terms = []
        for p in range(2):
            rows = slice(p * 2 * BLK, (p + 1) * 2 * BLK)
            q = q_ref[rows, c]
            inv, back = coef_ref[rows, 0:1], coef_ref[rows, 1:2]
            wide = att_ref[rows, c].astype(F32)
            sg = u_ref[rows, c].astype(F32) * gain
            norm_ref[rows, c] = (wide * inv * gain).astype(BF16)
            d = (inv * sg - wide * back).astype(BF16)
            s = dot(keys[p], q, NT) * (LOG2E * scale) + bias_ref[p]
            probs = jnp.exp2(s - lse_ref[h, :, rows])
            dp = dot(values[p], d, NT)
            inner = jnp.sum(probs * dp, 0, keepdims=True)
            ds = (probs * (dp - inner) * scale).astype(BF16)
            gq_ref[rows, c] = dot(ds, keys[p], TN).astype(BF16)
            terms.append((dot(ds, q, NN), dot(probs.astype(BF16), d, NN)))
        for part in range(2):
            a, b = terms[0][part], terms[1][part]
            eg_ref[0, part, :, c] = a[:BLK].astype(BF16)
            eg_ref[1, part, :, c] = b[3 * BLK:4 * BLK].astype(BF16)
            loc_ref[part, :, c] = jnp.concatenate(
                [a[BLK:2 * BLK], a[2 * BLK:4 * BLK] + b[:2 * BLK], b[2 * BLK:3 * BLK]], 0)
            gl1_ref[part, :, c] = jnp.concatenate(
                [b[4 * BLK:5 * BLK], a[4 * BLK:5 * BLK]], 0).astype(BF16)
        both = [terms[0][part][5 * BLK:] + terms[1][part][5 * BLK:] for part in range(2)]
        for k, (n, g) in enumerate(zip(FAR, (g2, g3, g4, g5))):
            m = BLK // n
            parts = [x[k * BLK:(k + 1) * BLK].reshape(n, m, HEAD_WIDTH) for x in both]
            g[:, :, c] = jnp.concatenate(parts, 1).astype(BF16)


def combine_kernel(count, loc_ref, gl1_ref, r2, r3, r4, r5, er_ref, gk_ref, gv_ref):
    me = lax.axis_index("seq")
    row_count, span = gk_ref.shape
    flags = (me > 0, me < count - 1)
    sizes = [ref.shape[0] * ref.shape[1] // 2 for ref in (r2, r3, r4, r5)]
    width = 2 * BLK + sum(sizes)
    row = lax.broadcasted_iota(jnp.int32, (row_count, width), 0)
    col = lax.broadcasted_iota(jnp.int32, (row_count, width), 1)
    mat = jnp.where((col < 2 * BLK) & (row // 2 == col), 0.5, 0.0)
    for k, n in enumerate(FAR):
        first = 2 * BLK + sum(sizes[:k])
        m = BLK // n
        inside = (col >= first) & (col < first + sizes[k])
        mat += jnp.where(inside & (row // (4 * n) == (col - first) % m), 0.25 / n, 0.0)
    mat = mat.astype(BF16)
    for part, out in enumerate((gk_ref, gv_ref)):
        far = [gl1_ref[part]]
        for n, ref in zip(FAR, (r2, r3, r4, r5)):
            m = BLK // n
            if m >= 16:
                far.append(ref[:, part * m:(part + 1) * m, :].reshape(-1, span))
            else:
                wide = ref[...].astype(F32)
                far.append(wide[:, part * m:(part + 1) * m].reshape(-1, span).astype(BF16))
        total = loc_ref[part] + dot(mat, jnp.concatenate(far, 0), NN)
        low = jnp.where(flags[0], er_ref[0, part].astype(F32), 0.0)
        high = jnp.where(flags[1], er_ref[1, part].astype(F32), 0.0)
        out[:BLK] = (total[:BLK] + low).astype(BF16)
        out[BLK:row_count - BLK] = total[BLK:row_count - BLK].astype(BF16)
        out[row_count - BLK:] = (total[row_count - BLK:] + high).astype(BF16)


def score_bias(seq_index, seq_count):
    key = jnp.arange(4 * BLK)[None, :, None] // BLK
    query = jnp.arange(2 * BLK)[None, None, :] // BLK
    pair = jnp.arange(2)[:, None, None]
    block = seq_index * 4 + 2 * pair + key - 1
    valid = (key >= query) & (key <= query + 2) & (block >= 0) & (block < 4 * seq_count)
    band = jnp.where(valid, 0.0, -1e30).astype(F32)
    levels = jnp.repeat(jnp.arange(1, LEV + 1).astype(F32), BLK)[None, :, None]
    return jnp.concatenate([band, jnp.broadcast_to(levels, (2, LEV * BLK, 2 * BLK))], 1)


def body(queries, keys_in, values_in, gain, upstream):
    rows, cols = queries.shape
    heads = cols // HEAD_WIDTH
    me = lax.axis_index("seq")
    count = lax.axis_size("seq")
    shape = jax.ShapeDtypeStruct
    any_spec = pl.BlockSpec(memory_space=pl.ANY)
    vmem = pl.BlockSpec(memory_space=pltpu.VMEM)
    pieces = piece_shapes(cols)
    piece_out = [shape(s, BF16) for s in pieces]
    edge_out = shape((2, 2, BLK, cols), BF16)
    limit = 48 * 1024 * 1024

    l1, *recv = pl.pallas_call(
        functools.partial(gather_kernel, count),
        out_shape=[shape((2, rows // 2, cols), BF16)] + piece_out + [edge_out],
        in_specs=[vmem] * 2,
        out_specs=[vmem] + [any_spec] * 5,
        scratch_shapes=[pltpu.VMEM(s[1:], BF16) for s in pieces] + sem_shapes(),
        compiler_params=pltpu.CompilerParams(
            collective_id=0, has_side_effects=True, vmem_limit_bytes=limit),
        name="gather_tiles",
    )(keys_in, values_in)
    bias = score_bias(me, count)
    gain2 = gain.reshape(1, cols)

    step = HEADS_STEP * HEAD_WIDTH
    grid = (heads // HEADS_STEP,)
    flat = lambda n: pl.BlockSpec((n, step), lambda i: (0, i))
    cube = lambda a, b: pl.BlockSpec((a, b, step), lambda i: (0, 0, i))
    quad = pl.BlockSpec((2, 2, BLK, step), lambda i: (0, 0, 0, i))
    fixed = lambda s: pl.BlockSpec(s, lambda i: (0,) * len(s))
    piece_specs = [cube(s[0], s[1]) for s in pieces]
    lse_spec = pl.BlockSpec((HEADS_STEP, 1, rows), lambda i: (i, 0, 0))
    shared = [flat(rows)] * 4 + [flat(1), fixed(bias.shape), cube(2, rows // 2)] + piece_specs + [quad]
    params = pltpu.CompilerParams(vmem_limit_bytes=limit)
    common = (queries, keys_in, values_in, upstream, gain2, bias, l1, *recv)
    att, lse, stat = pl.pallas_call(
        functools.partial(forward_kernel, count),
        grid=grid,
        out_shape=[shape((rows, cols), BF16), shape((heads, 1, rows), F32),
                   shape((2, rows, HEAD_WIDTH), F32)],
        in_specs=shared,
        out_specs=[flat(rows), lse_spec, fixed((2, rows, HEAD_WIDTH))],
        compiler_params=params,
        name="attend",
    )(*common)

    sums = jnp.sum(stat, -1)
    parts = lax.axis_size("head")
    total = sums
    for shift in range(1, parts):
        total = total + lax.ppermute(
            sums, "head", [(i, (i + shift) % parts) for i in range(parts)])
    columns = cols * parts
    inv = lax.rsqrt(total[0] / columns + EPSILON)
    coef = jnp.stack([inv, inv * inv * inv * total[1] / columns], 1)

    normed, gq, loc, gl1, *grads = pl.pallas_call(
        functools.partial(backward_kernel, count),
        grid=grid,
        out_shape=[shape((rows, cols), BF16)] * 2
        + [shape((2, rows, cols), F32), shape((2, rows // 2, cols), BF16)]
        + piece_out + [edge_out],
        in_specs=shared + [flat(rows), lse_spec, fixed((rows, 2))],
        out_specs=[flat(rows)] * 2 + [cube(2, rows), cube(2, rows // 2)] + piece_specs + [quad],
        compiler_params=params,
        name="differentiate",
    )(*common, att, lse, coef)

    summed = [(max(1, s[0] // 2),) + s[1:] for s in pieces]
    halves = [pltpu.VMEM(s[:2] + (cols // 2,), BF16) for s in pieces[1:]]
    back = pl.pallas_call(
        functools.partial(send_kernel, count),
        out_shape=[shape(s, BF16) for s in summed] + [edge_out],
        in_specs=[any_spec] * 5,
        out_specs=[any_spec] * 5,
        scratch_shapes=halves * 2 + [pltpu.SemaphoreType.DMA((LEV - 1,))] + sem_shapes(),
        compiler_params=pltpu.CompilerParams(
            collective_id=1, has_side_effects=True, vmem_limit_bytes=limit),
        name="send_terms",
    )(*grads)

    gk, gv = pl.pallas_call(
        functools.partial(combine_kernel, count),
        grid=grid,
        out_shape=[shape((rows, cols), BF16)] * 2,
        in_specs=[cube(2, rows), cube(2, rows // 2)]
        + [cube(s[0], s[1]) for s in summed] + [quad],
        out_specs=[flat(rows)] * 2,
        compiler_params=params,
        name="combine",
    )(loc, gl1, *back)
    return normed, gq, gk, gv


def solution(mesh):
    spec = P("seq", "head")
    return jax.shard_map(
        body,
        mesh=mesh,
        in_specs=(spec, spec, spec, P("head"), spec),
        out_specs=(spec,) * 4,
        check_vma=False,
    )
```

```python
import functools
import jax
import jax.numpy as jnp
from jax import lax
from jax.experimental import pallas as pl
from jax.experimental.pallas import tpu as pltpu
from jax.sharding import PartitionSpec as P

HEAD_WIDTH = 128
BLK = 64
LEV = 5
EPSILON = 1e-06
LOG2E = 1.4426950408889634
MESH = pl.DeviceIdType.MESH
HEADS_STEP = 4
FAR = tuple(1 << k for k in range(LEV - 1))
F32, BF16 = jnp.float32, jnp.bfloat16
NN = (((1,), (0,)), ((), ()))
NT = (((1,), (1,)), ((), ()))
TN = (((0,), (0,)), ((), ()))


def dot(a, b, dims):
    return lax.dot_general(a, b, dims, preferred_element_type=F32)


def piece_shapes(cols):
    return [(n, 2 * BLK // n, cols) for n in FAR]


def relations(me, count):
    peers = []
    for k, n in enumerate(FAR):
        g, o = me // n, me % n
        base = (g + 1 - 2 * (g % 2)) * n
        for r in range(n):
            peers.append((k, n, r, base + (o + r) % n, (o + r) % n, o))
    return peers, (me > 0, me < count - 1), (me - 1, me + 1)


def greet(peers, has, ids):
    barrier = pltpu.get_barrier_semaphore()
    for peer in peers:
        pl.semaphore_signal(barrier, inc=1, device_id={"seq": peer[3]}, device_id_type=MESH)
    for side in range(2):
        @pl.when(has[side])
        def _():
            pl.semaphore_signal(barrier, inc=1, device_id={"seq": ids[side]}, device_id_type=MESH)
    pl.semaphore_wait(
        barrier, len(peers) + has[0].astype(jnp.int32) + has[1].astype(jnp.int32))


def exchange(me, count, edge_src, edge_dst, sems, run_far):
    send_edge, recv_edge = sems
    peers, has, ids = relations(me, count)
    greet(peers, has, ids)

    def edge_copy(side, part):
        return pltpu.make_async_remote_copy(
            src_ref=edge_src(side, part), dst_ref=edge_dst(1 - side, part),
            send_sem=send_edge.at[side, part], recv_sem=recv_edge.at[1 - side, part],
            device_id={"seq": ids[side]}, device_id_type=MESH)

    def edge_wait(side, part):
        return pltpu.make_async_remote_copy(
            src_ref=edge_src(side, part), dst_ref=edge_dst(side, part),
            send_sem=send_edge.at[side, part], recv_sem=recv_edge.at[side, part],
            device_id={"seq": ids[side]}, device_id_type=MESH)

    for side in range(2):
        @pl.when(has[side])
        def _():
            for part in range(2):
                edge_copy(side, part).start()
    run_far(peers)
    for side in range(2):
        @pl.when(has[side])
        def _():
            for part in range(2):
                edge_wait(side, part).wait_send()
                edge_wait(side, part).wait_recv()


def remote(src, dst, sems, index, device):
    return pltpu.make_async_remote_copy(
        src_ref=src, dst_ref=dst,
        send_sem=sems[0] if index is None else sems[0].at[index],
        recv_sem=sems[1] if index is None else sems[1].at[index],
        device_id={"seq": device}, device_id_type=MESH)


def columns_of(core, half):
    return pl.ds(pl.multiple_of(core * half, HEAD_WIDTH), half)


def sem_shapes():
    total = sum(FAR)
    return [pltpu.SemaphoreType.DMA((total,))] * 4 + [
            pltpu.SemaphoreType.DMA((2, 2)), pltpu.SemaphoreType.DMA((2, 2))]


def halve(x):
    n = x.shape[0]
    row = lax.broadcasted_iota(jnp.int32, (n // 2, n), 0)
    col = lax.broadcasted_iota(jnp.int32, (n // 2, n), 1)
    mat = jnp.where((col == 2 * row) | (col == 2 * row + 1), 0.5, 0.0).astype(BF16)
    return dot(mat, x, NN)


def gather_kernel(count, k_ref, v_ref, l1_ref, r2, r3, r4, r5, edge_ref,
                  s2, s3, s4, s5, *sems):
    me = lax.axis_index("seq")
    rows, cols = k_ref.shape
    far_scr, far_out = (s2, s3, s4, s5), (r2, r3, r4, r5)
    width = 4 * HEAD_WIDTH

    def prepare():
        def step(i, _):
            c = pl.ds(pl.multiple_of(i * width, width), width)
            for part, ref in enumerate((k_ref, v_ref)):
                level = halve(ref[:, c]).astype(BF16)
                l1_ref[part, :, c] = level
                for scr, n in zip((s2, s3, s4), FAR):
                    level = halve(level).astype(BF16)
                    m = BLK // n
                    scr[part * m:(part + 1) * m, c] = level
            last = jnp.concatenate(
                [halve(s4[:16, c]), halve(s4[16:, c])], 0)
            s5[:, c] = last.astype(BF16)
            return 0
        lax.fori_loop(0, cols // width, step, 0)

    def edge_src(side, part):
        ref = (k_ref, v_ref)[part]
        return ref.at[pl.ds(0, BLK)] if side == 0 else ref.at[pl.ds(rows - BLK, BLK)]

    half = cols // 2
    core = me % 2
    mine = columns_of(core, half)

    def run_far(peers):
        prepare()
        order = peers[::-1]
        copies = []
        for k, n, r, dest, t, o in order:
            src, dst = far_scr[k], far_out[k].at[o]
            if n > 1:
                part = columns_of(t % 2, half)
                src, dst = src.at[:, part], dst.at[:, part]
            copies.append(remote(src, dst, sems[:2], n - 1 + r, dest))
            copies[-1].start()
        swaps = []
        for copy, (k, n, r, dest, t, o) in zip(copies, order):
            if n > 1:
                slot = far_out[k].at[(o + n - r) % n, :, mine]
                pltpu.make_async_remote_copy(
                    src_ref=slot, dst_ref=slot, send_sem=sems[0].at[n - 1 + r],
                    recv_sem=sems[1].at[n - 1 + r],
                    device_id={"seq": dest}, device_id_type=MESH).wait_recv()
                swaps.append(remote(slot, slot, sems[2:4], n - 1 + r, me + 1 - 2 * core))
                swaps[-1].start()
                copy.wait_send()
            else:
                copy.wait()
        for k, n, r, dest, t, o in order:
            if n > 1:
                theirs = (me + 1 - 2 * core) % n
                slot = far_out[k].at[(theirs + n - r) % n, :, columns_of(1 - core, half)]
                remote(slot, slot, sems[2:4], n - 1 + r, me + 1 - 2 * core).wait_recv()
        for swap in swaps:
            swap.wait_send()

    exchange(me, count, edge_src, lambda side, part: edge_ref.at[side, part], sems[4:], run_far)


def keep(x, flag):
    return jnp.where(flag, x.astype(F32), 0.0).astype(BF16)


def load_sets(me, count, c, k_ref, v_ref, l1_ref, far_refs, edge_ref):
    sets = []
    for part, ref in enumerate((k_ref, v_ref)):
        x = ref[:, c]
        low = keep(edge_ref[0, part, :, c], me > 0)
        high = keep(edge_ref[1, part, :, c], me < count - 1)
        far = []
        for n, far_ref in zip(FAR, far_refs):
            m = BLK // n
            if m >= 16:
                far.append(far_ref[:, part * m:(part + 1) * m, c].reshape(BLK, HEAD_WIDTH))
            else:
                wide = far_ref[:, :, c].astype(F32)
                far.append(wide[:, part * m:(part + 1) * m].reshape(BLK, HEAD_WIDTH).astype(BF16))
        sets.append((
            jnp.concatenate([low, x[:3 * BLK], l1_ref[part, BLK:, c]] + far, 0),
            jnp.concatenate([x[BLK:], high, l1_ref[part, :BLK, c]] + far, 0)))
    return sets


def forward_kernel(count, q_ref, k_ref, v_ref, u_ref, gain_ref, bias_ref, l1_ref,
                   r2, r3, r4, r5, edge_ref, att_ref, lse_ref, stat_ref):
    me = lax.axis_index("seq")

    @pl.when(pl.program_id(0) == 0)
    def _():
        stat_ref[...] = jnp.zeros_like(stat_ref)

    for h in range(HEADS_STEP):
        c = slice(h * HEAD_WIDTH, (h + 1) * HEAD_WIDTH)
        keys, values = load_sets(me, count, c, k_ref, v_ref, l1_ref, (r2, r3, r4, r5), edge_ref)
        gain = gain_ref[:, c].astype(F32)
        for p in range(2):
            rows = slice(p * 2 * BLK, (p + 1) * 2 * BLK)
            s = dot(keys[p], q_ref[rows, c], NT) * (LOG2E * HEAD_WIDTH ** -0.5) + bias_ref[p]
            top = jnp.max(s, 0, keepdims=True)
            e = jnp.exp2(s - top)
            total = jnp.sum(e, 0, keepdims=True)
            low = (e * (1.0 / total)).astype(BF16)
            lse_ref[h, :, rows] = top + jnp.log2(total)
            att = dot(low, values[p], TN).astype(BF16)
            att_ref[rows, c] = att
            wide = att.astype(F32)
            sg = u_ref[rows, c].astype(F32) * gain
            stat_ref[0, rows, :] += wide * wide
            stat_ref[1, rows, :] += sg * wide


def backward_kernel(count, q_ref, k_ref, v_ref, u_ref, gain_ref, bias_ref, l1_ref,
                    r2, r3, r4, r5, edge_ref, att_ref, lse_ref, coef_ref,
                    norm_ref, gq_ref, loc_ref, gl1_ref, g2, g3, g4, g5, eg_ref):
    me = lax.axis_index("seq")
    scale = HEAD_WIDTH ** -0.5
    for h in range(HEADS_STEP):
        c = slice(h * HEAD_WIDTH, (h + 1) * HEAD_WIDTH)
        keys, values = load_sets(me, count, c, k_ref, v_ref, l1_ref, (r2, r3, r4, r5), edge_ref)
        gain = gain_ref[:, c].astype(F32)
        terms = []
        for p in range(2):
            rows = slice(p * 2 * BLK, (p + 1) * 2 * BLK)
            q = q_ref[rows, c]
            inv, back = coef_ref[rows, 0:1], coef_ref[rows, 1:2]
            wide = att_ref[rows, c].astype(F32)
            sg = u_ref[rows, c].astype(F32) * gain
            norm_ref[rows, c] = (wide * inv * gain).astype(BF16)
            d = (inv * sg - wide * back).astype(BF16)
            s = dot(keys[p], q, NT) * (LOG2E * scale) + bias_ref[p]
            probs = jnp.exp2(s - lse_ref[h, :, rows])
            dp = dot(values[p], d, NT)
            inner = jnp.sum(probs * dp, 0, keepdims=True)
            ds = (probs * (dp - inner) * scale).astype(BF16)
            gq_ref[rows, c] = dot(ds, keys[p], TN).astype(BF16)
            terms.append((dot(ds, q, NN), dot(probs.astype(BF16), d, NN)))
        for part in range(2):
            a, b = terms[0][part], terms[1][part]
            eg_ref[0, part, :, c] = a[:BLK].astype(BF16)
            eg_ref[1, part, :, c] = b[3 * BLK:4 * BLK].astype(BF16)
            loc_ref[part, :, c] = jnp.concatenate(
                [a[BLK:2 * BLK], a[2 * BLK:4 * BLK] + b[:2 * BLK], b[2 * BLK:3 * BLK]], 0)
            gl1_ref[part, :, c] = jnp.concatenate(
                [b[4 * BLK:5 * BLK], a[4 * BLK:5 * BLK]], 0).astype(BF16)
        both = [terms[0][part][5 * BLK:] + terms[1][part][5 * BLK:] for part in range(2)]
        for k, (n, g) in enumerate(zip(FAR, (g2, g3, g4, g5))):
            m = BLK // n
            parts = [x[k * BLK:(k + 1) * BLK].reshape(n, m, HEAD_WIDTH) for x in both]
            g[:, :, c] = jnp.concatenate(parts, 1).astype(BF16)


def derive_send_kernel(count, steps, *refs):
    ins, outs = refs[:15], refs[15:19]
    dst, er = refs[19:23], refs[23]
    g, eg, own, came = refs[24:28], refs[28], (None,) + refs[29:32], (None,) + refs[32:35]
    far_sems, swap_sems, edge_sems = refs[35:37], refs[37:39], refs[39:41]
    me = lax.axis_index("seq")
    i = pl.program_id(0)
    step = HEADS_STEP * HEAD_WIDTH
    half = step // 2
    core = me % 2
    mate = me + 1 - 2 * core
    peers, has, ids = relations(me, count)

    @pl.when(i == 0)
    def _():
        greet(peers, has, ids)

    backward_kernel(count, *ins, *outs, *[ref.at[i] for ref in g], eg.at[i])

    def chunk(j):
        return pl.ds(pl.multiple_of(j * step, HEAD_WIDTH), step)

    def edge(j, side, slot):
        return remote(eg.at[j, side], er.at[slot, :, :, chunk(j)],
                      (edge_sems[0].at[j, side], edge_sems[1].at[j, slot]), None, ids[side])

    def swap(j, k):
        return remote(g[k].at[j, :, :, columns_of(1 - core, half)], came[k].at[j],
                      (swap_sems[0].at[j, k], swap_sems[1].at[j, k]), None, mate)

    def far(j, peer):
        k, n, r, dest, t, o = peer
        sems = (far_sems[0].at[j, n - 1 + r], far_sems[1].at[j, n - 1 + r])
        if k == 0:
            return remote(g[0].at[j, t], dst[0].at[o, :, chunk(j)], sems, None, dest)
        place = pl.ds(pl.multiple_of(j * step + core * half, HEAD_WIDTH), half)
        return remote(own[k].at[j, t], dst[k].at[o // 2, :, place], sems, None, dest)

    for k in (3, 2, 1):
        swap(i, k).start()
    for side in range(2):
        @pl.when(has[side])
        def _():
            edge(i, side, 1 - side).start()
    far(i, peers[0]).start()

    def send_sums(j):
        for level in (3, 2, 1):
            swap(j, level).wait()
            mine = g[level][j, :, :, columns_of(core, half)].astype(F32)
            own[level][j] = (mine + came[level][j].astype(F32)).astype(BF16)
            for peer in peers:
                if peer[0] == level:
                    far(j, peer).start()

    @pl.when(i > 0)
    def _():
        send_sums(i - 1)

    @pl.when(i == steps - 1)
    def _():
        send_sums(i)

        def finish(j, _):
            for peer in peers:
                far(j, peer).wait()
            for side in range(2):
                @pl.when(has[side])
                def _():
                    edge(j, side, 1 - side).wait_send()
                    edge(j, side, side).wait_recv()
            return 0
        lax.fori_loop(0, steps, finish, 0)


def combine_kernel(count, loc_ref, gl1_ref, r2, r3, r4, r5, er_ref, gk_ref, gv_ref):
    me = lax.axis_index("seq")
    row_count, span = gk_ref.shape
    flags = (me > 0, me < count - 1)
    sizes = [ref.shape[0] * ref.shape[1] // 2 for ref in (r2, r3, r4, r5)]
    width = 2 * BLK + sum(sizes)
    row = lax.broadcasted_iota(jnp.int32, (row_count, width), 0)
    col = lax.broadcasted_iota(jnp.int32, (row_count, width), 1)
    mat = jnp.where((col < 2 * BLK) & (row // 2 == col), 0.5, 0.0)
    for k, n in enumerate(FAR):
        first = 2 * BLK + sum(sizes[:k])
        m = BLK // n
        inside = (col >= first) & (col < first + sizes[k])
        mat += jnp.where(inside & (row // (4 * n) == (col - first) % m), 0.25 / n, 0.0)
    mat = mat.astype(BF16)
    for part, out in enumerate((gk_ref, gv_ref)):
        far = [gl1_ref[part]]
        for n, ref in zip(FAR, (r2, r3, r4, r5)):
            m = BLK // n
            if m >= 16:
                far.append(ref[:, part * m:(part + 1) * m, :].reshape(-1, span))
            else:
                wide = ref[...].astype(F32)
                far.append(wide[:, part * m:(part + 1) * m].reshape(-1, span).astype(BF16))
        total = loc_ref[part] + dot(mat, jnp.concatenate(far, 0), NN)
        low = jnp.where(flags[0], er_ref[0, part].astype(F32), 0.0)
        high = jnp.where(flags[1], er_ref[1, part].astype(F32), 0.0)
        out[:BLK] = (total[:BLK] + low).astype(BF16)
        out[BLK:row_count - BLK] = total[BLK:row_count - BLK].astype(BF16)
        out[row_count - BLK:] = (total[row_count - BLK:] + high).astype(BF16)


def score_bias(seq_index, seq_count):
    key = jnp.arange(4 * BLK)[None, :, None] // BLK
    query = jnp.arange(2 * BLK)[None, None, :] // BLK
    pair = jnp.arange(2)[:, None, None]
    block = seq_index * 4 + 2 * pair + key - 1
    valid = (key >= query) & (key <= query + 2) & (block >= 0) & (block < 4 * seq_count)
    band = jnp.where(valid, 0.0, -1e30).astype(F32)
    levels = jnp.repeat(jnp.arange(1, LEV + 1).astype(F32), BLK)[None, :, None]
    return jnp.concatenate([band, jnp.broadcast_to(levels, (2, LEV * BLK, 2 * BLK))], 1)


def body(queries, keys_in, values_in, gain, upstream):
    rows, cols = queries.shape
    heads = cols // HEAD_WIDTH
    me = lax.axis_index("seq")
    count = lax.axis_size("seq")
    shape = jax.ShapeDtypeStruct
    any_spec = pl.BlockSpec(memory_space=pl.ANY)
    vmem = pl.BlockSpec(memory_space=pltpu.VMEM)
    pieces = piece_shapes(cols)
    piece_out = [shape(s, BF16) for s in pieces]
    edge_out = shape((2, 2, BLK, cols), BF16)
    limit = 48 * 1024 * 1024

    l1, *recv = pl.pallas_call(
        functools.partial(gather_kernel, count),
        out_shape=[shape((2, rows // 2, cols), BF16)] + piece_out + [edge_out],
        in_specs=[vmem] * 2,
        out_specs=[vmem] + [any_spec] * 5,
        scratch_shapes=[pltpu.VMEM(s[1:], BF16) for s in pieces] + sem_shapes(),
        compiler_params=pltpu.CompilerParams(
            collective_id=0, has_side_effects=True, vmem_limit_bytes=limit),
        name="gather_tiles",
    )(keys_in, values_in)
    bias = score_bias(me, count)
    gain2 = gain.reshape(1, cols)

    step = HEADS_STEP * HEAD_WIDTH
    grid = (heads // HEADS_STEP,)
    flat = lambda n: pl.BlockSpec((n, step), lambda i: (0, i))
    cube = lambda a, b: pl.BlockSpec((a, b, step), lambda i: (0, 0, i))
    quad = pl.BlockSpec((2, 2, BLK, step), lambda i: (0, 0, 0, i))
    fixed = lambda s: pl.BlockSpec(s, lambda i: (0,) * len(s))
    piece_specs = [cube(s[0], s[1]) for s in pieces]
    lse_spec = pl.BlockSpec((HEADS_STEP, 1, rows), lambda i: (i, 0, 0))
    shared = [flat(rows)] * 4 + [flat(1), fixed(bias.shape), cube(2, rows // 2)] + piece_specs + [quad]
    params = pltpu.CompilerParams(vmem_limit_bytes=limit)
    common = (queries, keys_in, values_in, upstream, gain2, bias, l1, *recv)
    att, lse, stat = pl.pallas_call(
        functools.partial(forward_kernel, count),
        grid=grid,
        out_shape=[shape((rows, cols), BF16), shape((heads, 1, rows), F32),
                   shape((2, rows, HEAD_WIDTH), F32)],
        in_specs=shared,
        out_specs=[flat(rows), lse_spec, fixed((2, rows, HEAD_WIDTH))],
        compiler_params=params,
        name="attend",
    )(*common)

    sums = jnp.sum(stat, -1)
    parts = lax.axis_size("head")
    total = sums
    for shift in range(1, parts):
        total = total + lax.ppermute(
            sums, "head", [(i, (i + shift) % parts) for i in range(parts)])
    columns = cols * parts
    inv = lax.rsqrt(total[0] / columns + EPSILON)
    coef = jnp.stack([inv, inv * inv * inv * total[1] / columns], 1)

    steps = grid[0]
    summed = [(max(1, s[0] // 2),) + s[1:] for s in pieces]
    chunks = [pltpu.VMEM((steps,) + s[:2] + (step,), BF16) for s in pieces]
    halves = [pltpu.VMEM((steps,) + s[:2] + (step // 2,), BF16) for s in pieces[1:]]
    dma = pltpu.SemaphoreType.DMA
    normed, gq, loc, gl1, *back = pl.pallas_call(
        functools.partial(derive_send_kernel, count, steps),
        grid=grid,
        out_shape=[shape((rows, cols), BF16)] * 2
        + [shape((2, rows, cols), F32), shape((2, rows // 2, cols), BF16)]
        + [shape(s, BF16) for s in summed] + [edge_out],
        in_specs=shared + [flat(rows), lse_spec, fixed((rows, 2))],
        out_specs=[flat(rows)] * 2 + [cube(2, rows), cube(2, rows // 2)] + [any_spec] * 5,
        scratch_shapes=chunks + [pltpu.VMEM((steps, 2, 2, BLK, step), BF16)] + halves * 2
        + [dma((steps, sum(FAR)))] * 2 + [dma((steps, LEV - 1))] * 2 + [dma((steps, 2))] * 2,
        compiler_params=pltpu.CompilerParams(
            collective_id=1, has_side_effects=True, vmem_limit_bytes=limit),
        name="differentiate_and_send",
    )(*common, att, lse, coef)

    gk, gv = pl.pallas_call(
        functools.partial(combine_kernel, count),
        grid=grid,
        out_shape=[shape((rows, cols), BF16)] * 2,
        in_specs=[cube(2, rows), cube(2, rows // 2)]
        + [cube(s[0], s[1]) for s in summed] + [quad],
        out_specs=[flat(rows)] * 2,
        compiler_params=params,
        name="combine",
    )(loc, gl1, *back)
    return normed, gq, gk, gv


def solution(mesh):
    spec = P("seq", "head")
    return jax.shard_map(
        body,
        mesh=mesh,
        in_specs=(spec, spec, spec, P("head"), spec),
        out_specs=(spec,) * 4,
        check_vma=False,
    )
```

```python
import functools
import jax
import jax.numpy as jnp
from jax import lax
from jax.experimental import pallas as pl
from jax.experimental.pallas import tpu as pltpu
from jax.sharding import PartitionSpec as P

HEAD_WIDTH = 128
BLK = 64
LEV = 5
EPSILON = 1e-06
LOG2E = 1.4426950408889634
MESH = pl.DeviceIdType.MESH
HEADS_STEP = 4
FAR = tuple(1 << k for k in range(LEV - 1))
F32, BF16 = jnp.float32, jnp.bfloat16
NN = (((1,), (0,)), ((), ()))
NT = (((1,), (1,)), ((), ()))
TN = (((0,), (0,)), ((), ()))


def dot(a, b, dims):
    return lax.dot_general(a, b, dims, preferred_element_type=F32)


def piece_shapes(cols):
    return [(n, 2 * BLK // n, cols) for n in FAR]


def relations(me, count):
    peers = []
    for k, n in enumerate(FAR):
        g, o = me // n, me % n
        base = (g + 1 - 2 * (g % 2)) * n
        for r in range(n):
            peers.append((k, n, r, base + (o + r) % n, (o + r) % n, o))
    return peers, (me > 0, me < count - 1), (me - 1, me + 1)


def greet(peers, has, ids):
    barrier = pltpu.get_barrier_semaphore()
    for peer in peers:
        pl.semaphore_signal(barrier, inc=1, device_id={"seq": peer[3]}, device_id_type=MESH)
    for side in range(2):
        @pl.when(has[side])
        def _():
            pl.semaphore_signal(barrier, inc=1, device_id={"seq": ids[side]}, device_id_type=MESH)
    pl.semaphore_wait(
        barrier, len(peers) + has[0].astype(jnp.int32) + has[1].astype(jnp.int32))


def remote(src, dst, sems, index, device):
    return pltpu.make_async_remote_copy(
        src_ref=src, dst_ref=dst,
        send_sem=sems[0] if index is None else sems[0].at[index],
        recv_sem=sems[1] if index is None else sems[1].at[index],
        device_id={"seq": device}, device_id_type=MESH)


def columns_of(core, half):
    return pl.ds(pl.multiple_of(core * half, HEAD_WIDTH), half)


def halve(x):
    n = x.shape[0]
    row = lax.broadcasted_iota(jnp.int32, (n // 2, n), 0)
    col = lax.broadcasted_iota(jnp.int32, (n // 2, n), 1)
    mat = jnp.where((col == 2 * row) | (col == 2 * row + 1), 0.5, 0.0).astype(BF16)
    return dot(mat, x, NN)


def keep(x, flag):
    return jnp.where(flag, x.astype(F32), 0.0).astype(BF16)


def load_sets(me, count, c, k_ref, v_ref, l1_ref, far_refs, edge_ref):
    sets = []
    for part, ref in enumerate((k_ref, v_ref)):
        x = ref[:, c]
        low = keep(edge_ref[0, part, :, c], me > 0)
        high = keep(edge_ref[1, part, :, c], me < count - 1)
        far = []
        for n, far_ref in zip(FAR, far_refs):
            m = BLK // n
            if m >= 16:
                far.append(far_ref[:, part * m:(part + 1) * m, c].reshape(BLK, HEAD_WIDTH))
            else:
                wide = far_ref[:, :, c].astype(F32)
                far.append(wide[:, part * m:(part + 1) * m].reshape(BLK, HEAD_WIDTH).astype(BF16))
        sets.append((
            jnp.concatenate([low, x[:3 * BLK], l1_ref[part, BLK:, c]] + far, 0),
            jnp.concatenate([x[BLK:], high, l1_ref[part, :BLK, c]] + far, 0)))
    return sets


def forward_kernel(count, q_ref, k_ref, v_ref, u_ref, gain_ref, bias_ref, l1_ref,
                   r2, r3, r4, r5, edge_ref, att_ref, lse_ref, stat_ref):
    me = lax.axis_index("seq")

    @pl.when(pl.program_id(0) == 0)
    def _():
        stat_ref[...] = jnp.zeros_like(stat_ref)

    for h in range(HEADS_STEP):
        c = slice(h * HEAD_WIDTH, (h + 1) * HEAD_WIDTH)
        keys, values = load_sets(me, count, c, k_ref, v_ref, l1_ref, (r2, r3, r4, r5), edge_ref)
        gain = gain_ref[:, c].astype(F32)
        for p in range(2):
            rows = slice(p * 2 * BLK, (p + 1) * 2 * BLK)
            s = dot(keys[p], q_ref[rows, c], NT) * (LOG2E * HEAD_WIDTH ** -0.5) + bias_ref[p]
            top = jnp.max(s, 0, keepdims=True)
            e = jnp.exp2(s - top)
            total = jnp.sum(e, 0, keepdims=True)
            low = (e * (1.0 / total)).astype(BF16)
            lse_ref[h, :, rows] = top + jnp.log2(total)
            att = dot(low, values[p], TN).astype(BF16)
            att_ref[rows, c] = att
            wide = att.astype(F32)
            sg = u_ref[rows, c].astype(F32) * gain
            stat_ref[0, rows, :] += wide * wide
            stat_ref[1, rows, :] += sg * wide


def gather_attend_kernel(count, steps, *refs):
    q_ref, k_ref, v_ref, u_ref, gain_ref, bias_ref = refs[:6]
    stats, outs = refs[6:9], refs[9:15]
    l1, recv, er, coarse = refs[15], refs[16:20], refs[20], refs[21:25]
    far_sems, swap_sems, edge_sems, out_sem = refs[25:27], refs[27:29], refs[29:31], refs[31]
    me = lax.axis_index("seq")
    i = pl.program_id(0)
    rows = k_ref.shape[0]
    step = HEADS_STEP * HEAD_WIDTH
    half = step // 2
    core = me % 2
    mate = me + 1 - 2 * core
    peers, has, ids = relations(me, count)
    order = peers[::-1]

    def chunk(j):
        return pl.ds(pl.multiple_of(j * step, HEAD_WIDTH), step)

    def edge(j, side, part, slot):
        ref = (k_ref, v_ref)[part]
        src = ref.at[pl.ds(side * (rows - BLK), BLK), chunk(j)]
        return remote(src, er.at[j, slot, part],
                      (edge_sems[0].at[j, side, part], edge_sems[1].at[j, slot, part]),
                      None, ids[side])

    def far(j, peer):
        k, n, r, dest, t, o = peer
        sems = (far_sems[0].at[j, n - 1 + r], far_sems[1].at[j, n - 1 + r])
        if n == 1:
            return remote(coarse[0].at[j], recv[0].at[j, 0], sems, None, dest)
        part = columns_of(t % 2, half)
        return remote(coarse[k].at[j, :, part], recv[k].at[j, o, :, part], sems, None, dest)

    def swap(j, peer, owner, side, sems):
        k, n, r = peer[:3]
        slot = recv[k].at[j, (owner % n + n - r) % n, :, columns_of(side, half)]
        return remote(slot, slot,
                      (sems[0].at[j, n - 1 + r], sems[1].at[j, n - 1 + r]), None, mate)

    def stores(j):
        pairs = [(l1.at[j], outs[0].at[:, :, chunk(j)])]
        pairs += [(recv[k].at[j], outs[1 + k].at[:, :, chunk(j)]) for k in range(len(FAR))]
        pairs.append((er.at[j], outs[5].at[:, :, :, chunk(j)]))
        return [pltpu.make_async_copy(src, dst, out_sem.at[j, n])
                for n, (src, dst) in enumerate(pairs)]

    def send(j, _):
        for part, ref in enumerate((k_ref, v_ref)):
            level = halve(ref[:, chunk(j)]).astype(BF16)
            l1[j, part] = level
            for scr, n in zip(coarse[:3], FAR):
                level = halve(level).astype(BF16)
                m = BLK // n
                scr[j, part * m:(part + 1) * m] = level
        coarse[3][j] = jnp.concatenate(
            [halve(coarse[2][j, :16]), halve(coarse[2][j, 16:])], 0).astype(BF16)
        for peer in order:
            far(j, peer).start()
        for side in range(2):
            @pl.when(has[side])
            def _():
                for part in range(2):
                    edge(j, side, part, 1 - side).start()
        return 0

    def receive(j):
        for peer in order:
            if peer[1] == 1:
                far(j, peer).wait_recv()
            else:
                swap(j, peer, me, core, far_sems).wait_recv()
                swap(j, peer, me, core, swap_sems).start()

    @pl.when(i == 0)
    def _():
        greet(peers, has, ids)
        lax.fori_loop(0, steps, send, 0)
        receive(0)

    for peer in order:
        if peer[1] > 1:
            swap(i, peer, mate, 1 - core, swap_sems).wait_recv()
    for side in range(2):
        @pl.when(has[side])
        def _():
            for part in range(2):
                edge(i, side, part, side).wait_recv()
    for copy in stores(i):
        copy.start()
    here = chunk(i)
    forward_kernel(count, q_ref, k_ref.at[:, here], v_ref.at[:, here], u_ref, gain_ref,
                   bias_ref, l1.at[i], *[ref.at[i] for ref in recv], er.at[i], *stats)

    @pl.when(i < steps - 1)
    def _():
        receive(i + 1)

    @pl.when(i == steps - 1)
    def _():
        def finish(j, _):
            for peer in order:
                far(j, peer).wait_send()
                if peer[1] > 1:
                    swap(j, peer, me, core, swap_sems).wait_send()
            for side in range(2):
                @pl.when(has[side])
                def _():
                    for part in range(2):
                        edge(j, side, part, 1 - side).wait_send()
            for copy in stores(j):
                copy.wait()
            return 0
        lax.fori_loop(0, steps, finish, 0)


def backward_kernel(count, q_ref, k_ref, v_ref, u_ref, gain_ref, bias_ref, l1_ref,
                    r2, r3, r4, r5, edge_ref, att_ref, lse_ref, coef_ref,
                    norm_ref, gq_ref, loc_ref, gl1_ref, g2, g3, g4, g5, eg_ref):
    me = lax.axis_index("seq")
    scale = HEAD_WIDTH ** -0.5
    for h in range(HEADS_STEP):
        c = slice(h * HEAD_WIDTH, (h + 1) * HEAD_WIDTH)
        keys, values = load_sets(me, count, c, k_ref, v_ref, l1_ref, (r2, r3, r4, r5), edge_ref)
        gain = gain_ref[:, c].astype(F32)
        terms = []
        for p in range(2):
            rows = slice(p * 2 * BLK, (p + 1) * 2 * BLK)
            q = q_ref[rows, c]
            inv, back = coef_ref[rows, 0:1], coef_ref[rows, 1:2]
            wide = att_ref[rows, c].astype(F32)
            sg = u_ref[rows, c].astype(F32) * gain
            norm_ref[rows, c] = (wide * inv * gain).astype(BF16)
            d = (inv * sg - wide * back).astype(BF16)
            s = dot(keys[p], q, NT) * (LOG2E * scale) + bias_ref[p]
            probs = jnp.exp2(s - lse_ref[h, :, rows])
            dp = dot(values[p], d, NT)
            inner = jnp.sum(probs * dp, 0, keepdims=True)
            ds = (probs * (dp - inner) * scale).astype(BF16)
            gq_ref[rows, c] = dot(ds, keys[p], TN).astype(BF16)
            terms.append((dot(ds, q, NN), dot(probs.astype(BF16), d, NN)))
        for part in range(2):
            a, b = terms[0][part], terms[1][part]
            eg_ref[0, part, :, c] = a[:BLK].astype(BF16)
            eg_ref[1, part, :, c] = b[3 * BLK:4 * BLK].astype(BF16)
            loc_ref[part, :, c] = jnp.concatenate(
                [a[BLK:2 * BLK], a[2 * BLK:4 * BLK] + b[:2 * BLK], b[2 * BLK:3 * BLK]], 0)
            gl1_ref[part, :, c] = jnp.concatenate(
                [b[4 * BLK:5 * BLK], a[4 * BLK:5 * BLK]], 0).astype(BF16)
        both = [terms[0][part][5 * BLK:] + terms[1][part][5 * BLK:] for part in range(2)]
        for k, (n, g) in enumerate(zip(FAR, (g2, g3, g4, g5))):
            m = BLK // n
            parts = [x[k * BLK:(k + 1) * BLK].reshape(n, m, HEAD_WIDTH) for x in both]
            g[:, :, c] = jnp.concatenate(parts, 1).astype(BF16)


def derive_send_kernel(count, steps, *refs):
    ins, outs = refs[:15], refs[15:19]
    dst, er = refs[19:23], refs[23]
    g, eg, own, came = refs[24:28], refs[28], (None,) + refs[29:32], (None,) + refs[32:35]
    far_sems, swap_sems, edge_sems = refs[35:37], refs[37:39], refs[39:41]
    me = lax.axis_index("seq")
    i = pl.program_id(0)
    step = HEADS_STEP * HEAD_WIDTH
    half = step // 2
    core = me % 2
    mate = me + 1 - 2 * core
    peers, has, ids = relations(me, count)

    @pl.when(i == 0)
    def _():
        greet(peers, has, ids)

    backward_kernel(count, *ins, *outs, *[ref.at[i] for ref in g], eg.at[i])

    def chunk(j):
        return pl.ds(pl.multiple_of(j * step, HEAD_WIDTH), step)

    def edge(j, side, slot):
        return remote(eg.at[j, side], er.at[slot, :, :, chunk(j)],
                      (edge_sems[0].at[j, side], edge_sems[1].at[j, slot]), None, ids[side])

    def swap(j, k):
        return remote(g[k].at[j, :, :, columns_of(1 - core, half)], came[k].at[j],
                      (swap_sems[0].at[j, k], swap_sems[1].at[j, k]), None, mate)

    def far(j, peer):
        k, n, r, dest, t, o = peer
        sems = (far_sems[0].at[j, n - 1 + r], far_sems[1].at[j, n - 1 + r])
        if k == 0:
            return remote(g[0].at[j, t], dst[0].at[o, :, chunk(j)], sems, None, dest)
        place = pl.ds(pl.multiple_of(j * step + core * half, HEAD_WIDTH), half)
        return remote(own[k].at[j, t], dst[k].at[o // 2, :, place], sems, None, dest)

    for k in (3, 2, 1):
        swap(i, k).start()
    for side in range(2):
        @pl.when(has[side])
        def _():
            edge(i, side, 1 - side).start()
    far(i, peers[0]).start()

    def send_sums(j):
        for level in (3, 2, 1):
            swap(j, level).wait()
            mine = g[level][j, :, :, columns_of(core, half)].astype(F32)
            own[level][j] = (mine + came[level][j].astype(F32)).astype(BF16)
            for peer in peers:
                if peer[0] == level:
                    far(j, peer).start()

    @pl.when(i > 0)
    def _():
        send_sums(i - 1)

    @pl.when(i == steps - 1)
    def _():
        send_sums(i)

        def finish(j, _):
            for peer in peers:
                far(j, peer).wait()
            for side in range(2):
                @pl.when(has[side])
                def _():
                    edge(j, side, 1 - side).wait_send()
                    edge(j, side, side).wait_recv()
            return 0
        lax.fori_loop(0, steps, finish, 0)


def combine_kernel(count, loc_ref, gl1_ref, r2, r3, r4, r5, er_ref, gk_ref, gv_ref):
    me = lax.axis_index("seq")
    row_count, span = gk_ref.shape
    flags = (me > 0, me < count - 1)
    sizes = [ref.shape[0] * ref.shape[1] // 2 for ref in (r2, r3, r4, r5)]
    width = 2 * BLK + sum(sizes)
    row = lax.broadcasted_iota(jnp.int32, (row_count, width), 0)
    col = lax.broadcasted_iota(jnp.int32, (row_count, width), 1)
    mat = jnp.where((col < 2 * BLK) & (row // 2 == col), 0.5, 0.0)
    for k, n in enumerate(FAR):
        first = 2 * BLK + sum(sizes[:k])
        m = BLK // n
        inside = (col >= first) & (col < first + sizes[k])
        mat += jnp.where(inside & (row // (4 * n) == (col - first) % m), 0.25 / n, 0.0)
    mat = mat.astype(BF16)
    for part, out in enumerate((gk_ref, gv_ref)):
        far = [gl1_ref[part]]
        for n, ref in zip(FAR, (r2, r3, r4, r5)):
            m = BLK // n
            if m >= 16:
                far.append(ref[:, part * m:(part + 1) * m, :].reshape(-1, span))
            else:
                wide = ref[...].astype(F32)
                far.append(wide[:, part * m:(part + 1) * m].reshape(-1, span).astype(BF16))
        total = loc_ref[part] + dot(mat, jnp.concatenate(far, 0), NN)
        low = jnp.where(flags[0], er_ref[0, part].astype(F32), 0.0)
        high = jnp.where(flags[1], er_ref[1, part].astype(F32), 0.0)
        out[:BLK] = (total[:BLK] + low).astype(BF16)
        out[BLK:row_count - BLK] = total[BLK:row_count - BLK].astype(BF16)
        out[row_count - BLK:] = (total[row_count - BLK:] + high).astype(BF16)


def score_bias(seq_index, seq_count):
    key = jnp.arange(4 * BLK)[None, :, None] // BLK
    query = jnp.arange(2 * BLK)[None, None, :] // BLK
    pair = jnp.arange(2)[:, None, None]
    block = seq_index * 4 + 2 * pair + key - 1
    valid = (key >= query) & (key <= query + 2) & (block >= 0) & (block < 4 * seq_count)
    band = jnp.where(valid, 0.0, -1e30).astype(F32)
    levels = jnp.repeat(jnp.arange(1, LEV + 1).astype(F32), BLK)[None, :, None]
    return jnp.concatenate([band, jnp.broadcast_to(levels, (2, LEV * BLK, 2 * BLK))], 1)


def body(queries, keys_in, values_in, gain, upstream):
    rows, cols = queries.shape
    heads = cols // HEAD_WIDTH
    me = lax.axis_index("seq")
    count = lax.axis_size("seq")
    shape = jax.ShapeDtypeStruct
    any_spec = pl.BlockSpec(memory_space=pl.ANY)
    vmem = pl.BlockSpec(memory_space=pltpu.VMEM)
    pieces = piece_shapes(cols)
    piece_out = [shape(s, BF16) for s in pieces]
    edge_out = shape((2, 2, BLK, cols), BF16)
    limit = 48 * 1024 * 1024

    bias = score_bias(me, count)
    gain2 = gain.reshape(1, cols)

    step = HEADS_STEP * HEAD_WIDTH
    grid = (heads // HEADS_STEP,)
    flat = lambda n: pl.BlockSpec((n, step), lambda i: (0, i))
    cube = lambda a, b: pl.BlockSpec((a, b, step), lambda i: (0, 0, i))
    quad = pl.BlockSpec((2, 2, BLK, step), lambda i: (0, 0, 0, i))
    fixed = lambda s: pl.BlockSpec(s, lambda i: (0,) * len(s))
    piece_specs = [cube(s[0], s[1]) for s in pieces]
    lse_spec = pl.BlockSpec((HEADS_STEP, 1, rows), lambda i: (i, 0, 0))
    shared = [flat(rows)] * 4 + [flat(1), fixed(bias.shape), cube(2, rows // 2)] + piece_specs + [quad]
    params = pltpu.CompilerParams(vmem_limit_bytes=limit)
    steps = grid[0]
    dma = pltpu.SemaphoreType.DMA
    chunks = [pltpu.VMEM((steps,) + s[:2] + (step,), BF16) for s in pieces]
    edges = pltpu.VMEM((steps, 2, 2, BLK, step), BF16)
    att, lse, stat, l1, *recv = pl.pallas_call(
        functools.partial(gather_attend_kernel, count, steps),
        grid=grid,
        out_shape=[shape((rows, cols), BF16), shape((heads, 1, rows), F32),
                   shape((2, rows, HEAD_WIDTH), F32), shape((2, rows // 2, cols), BF16)]
        + piece_out + [edge_out],
        in_specs=[flat(rows), vmem, vmem, flat(rows), flat(1), fixed(bias.shape)],
        out_specs=[flat(rows), lse_spec, fixed((2, rows, HEAD_WIDTH))] + [any_spec] * 6,
        scratch_shapes=[pltpu.VMEM((steps, 2, rows // 2, step), BF16)] + chunks + [edges]
        + [pltpu.VMEM((steps, s[1], step), BF16) for s in pieces]
        + [dma((steps, sum(FAR)))] * 4 + [dma((steps, 2, 2))] * 2 + [dma((steps, 6))],
        compiler_params=pltpu.CompilerParams(
            collective_id=0, has_side_effects=True, vmem_limit_bytes=limit),
        name="gather_and_attend",
    )(queries, keys_in, values_in, upstream, gain2, bias)
    common = (queries, keys_in, values_in, upstream, gain2, bias, l1, *recv)

    sums = jnp.sum(stat, -1)
    parts = lax.axis_size("head")
    total = sums
    for shift in range(1, parts):
        total = total + lax.ppermute(
            sums, "head", [(i, (i + shift) % parts) for i in range(parts)])
    columns = cols * parts
    inv = lax.rsqrt(total[0] / columns + EPSILON)
    coef = jnp.stack([inv, inv * inv * inv * total[1] / columns], 1)

    summed = [(max(1, s[0] // 2),) + s[1:] for s in pieces]
    halves = [pltpu.VMEM((steps,) + s[:2] + (step // 2,), BF16) for s in pieces[1:]]
    normed, gq, loc, gl1, *back = pl.pallas_call(
        functools.partial(derive_send_kernel, count, steps),
        grid=grid,
        out_shape=[shape((rows, cols), BF16)] * 2
        + [shape((2, rows, cols), F32), shape((2, rows // 2, cols), BF16)]
        + [shape(s, BF16) for s in summed] + [edge_out],
        in_specs=shared + [flat(rows), lse_spec, fixed((rows, 2))],
        out_specs=[flat(rows)] * 2 + [cube(2, rows), cube(2, rows // 2)] + [any_spec] * 5,
        scratch_shapes=chunks + [edges] + halves * 2
        + [dma((steps, sum(FAR)))] * 2 + [dma((steps, LEV - 1))] * 2 + [dma((steps, 2))] * 2,
        compiler_params=pltpu.CompilerParams(
            collective_id=1, has_side_effects=True, vmem_limit_bytes=limit),
        name="differentiate_and_send",
    )(*common, att, lse, coef)

    gk, gv = pl.pallas_call(
        functools.partial(combine_kernel, count),
        grid=grid,
        out_shape=[shape((rows, cols), BF16)] * 2,
        in_specs=[cube(2, rows), cube(2, rows // 2)]
        + [cube(s[0], s[1]) for s in summed] + [quad],
        out_specs=[flat(rows)] * 2,
        compiler_params=params,
        name="combine",
    )(loc, gl1, *back)
    return normed, gq, gk, gv


def solution(mesh):
    spec = P("seq", "head")
    return jax.shard_map(
        body,
        mesh=mesh,
        in_specs=(spec, spec, spec, P("head"), spec),
        out_specs=(spec,) * 4,
        check_vma=False,
    )
```

```python
import functools
import jax
import jax.numpy as jnp
from jax import lax
from jax.experimental import pallas as pl
from jax.experimental.pallas import tpu as pltpu
from jax.sharding import PartitionSpec as P

HEAD_WIDTH = 128
BLK = 64
LEV = 5
EPSILON = 1e-06
LOG2E = 1.4426950408889634
MESH = pl.DeviceIdType.MESH
HEADS_STEP = 4
FAR = tuple(1 << k for k in range(LEV - 1))
F32, BF16 = jnp.float32, jnp.bfloat16
NN = (((1,), (0,)), ((), ()))
NT = (((1,), (1,)), ((), ()))
TN = (((0,), (0,)), ((), ()))


def dot(a, b, dims):
    return lax.dot_general(a, b, dims, preferred_element_type=F32)


def piece_shapes(cols):
    return [(n, 2 * BLK // n, cols) for n in FAR]


def relations(me, count):
    peers = []
    for k, n in enumerate(FAR):
        g, o = me // n, me % n
        base = (g + 1 - 2 * (g % 2)) * n
        for r in range(n):
            peers.append((k, n, r, base + (o + r) % n, (o + r) % n, o))
    return peers, (me > 0, me < count - 1), (me - 1, me + 1)


def greet(peers, has, ids):
    barrier = pltpu.get_barrier_semaphore()
    for peer in peers:
        pl.semaphore_signal(barrier, inc=1, device_id={"seq": peer[3]}, device_id_type=MESH)
    for side in range(2):
        @pl.when(has[side])
        def _():
            pl.semaphore_signal(barrier, inc=1, device_id={"seq": ids[side]}, device_id_type=MESH)
    pl.semaphore_wait(
        barrier, len(peers) + has[0].astype(jnp.int32) + has[1].astype(jnp.int32))


def remote(src, dst, sems, index, device):
    return pltpu.make_async_remote_copy(
        src_ref=src, dst_ref=dst,
        send_sem=sems[0] if index is None else sems[0].at[index],
        recv_sem=sems[1] if index is None else sems[1].at[index],
        device_id={"seq": device}, device_id_type=MESH)


def columns_of(core, half):
    return pl.ds(pl.multiple_of(core * half, HEAD_WIDTH), half)


def halve(x):
    n = x.shape[0]
    row = lax.broadcasted_iota(jnp.int32, (n // 2, n), 0)
    col = lax.broadcasted_iota(jnp.int32, (n // 2, n), 1)
    mat = jnp.where((col == 2 * row) | (col == 2 * row + 1), 0.5, 0.0).astype(BF16)
    return dot(mat, x, NN)


def keep(x, flag):
    return jnp.where(flag, x.astype(F32), 0.0).astype(BF16)


def load_sets(me, count, c, k_ref, v_ref, l1_ref, far_refs, edge_ref):
    sets = []
    for part, ref in enumerate((k_ref, v_ref)):
        x = ref[:, c]
        low = keep(edge_ref[0, part, :, c], me > 0)
        high = keep(edge_ref[1, part, :, c], me < count - 1)
        far = []
        for n, far_ref in zip(FAR, far_refs):
            m = BLK // n
            if m >= 16:
                far.append(far_ref[:, part * m:(part + 1) * m, c].reshape(BLK, HEAD_WIDTH))
            else:
                wide = far_ref[:, :, c].astype(F32)
                far.append(wide[:, part * m:(part + 1) * m].reshape(BLK, HEAD_WIDTH).astype(BF16))
        sets.append((
            jnp.concatenate([low, x[:3 * BLK], l1_ref[part, BLK:, c]] + far, 0),
            jnp.concatenate([x[BLK:], high, l1_ref[part, :BLK, c]] + far, 0)))
    return sets


def forward_kernel(count, q_ref, k_ref, v_ref, u_ref, gain_ref, bias_ref, l1_ref,
                   r2, r3, r4, r5, edge_ref, att_ref, lse_ref, stat_ref):
    me = lax.axis_index("seq")

    @pl.when(pl.program_id(0) == 0)
    def _():
        stat_ref[...] = jnp.zeros_like(stat_ref)

    for h in range(HEADS_STEP):
        c = slice(h * HEAD_WIDTH, (h + 1) * HEAD_WIDTH)
        keys, values = load_sets(me, count, c, k_ref, v_ref, l1_ref, (r2, r3, r4, r5), edge_ref)
        gain = gain_ref[:, c].astype(F32)
        for p in range(2):
            rows = slice(p * 2 * BLK, (p + 1) * 2 * BLK)
            s = dot(keys[p], q_ref[rows, c], NT) * (LOG2E * HEAD_WIDTH ** -0.5) + bias_ref[p]
            top = jnp.max(s, 0, keepdims=True)
            e = jnp.exp2(s - top)
            total = jnp.sum(e, 0, keepdims=True)
            low = (e * (1.0 / total)).astype(BF16)
            lse_ref[h, :, rows] = top + jnp.log2(total)
            att = dot(low, values[p], TN).astype(BF16)
            att_ref[rows, c] = att
            wide = att.astype(F32)
            sg = u_ref[rows, c].astype(F32) * gain
            stat_ref[0, rows, :] += wide * wide
            stat_ref[1, rows, :] += sg * wide


def gather_attend_kernel(count, steps, *refs):
    q_ref, k_ref, v_ref, u_ref, gain_ref, bias_ref = refs[:6]
    stats, outs = refs[6:9], refs[9:15]
    l1, recv, er, coarse = refs[15], refs[16:20], refs[20], refs[21:25]
    far_sems, swap_sems, edge_sems, out_sem = refs[25:27], refs[27:29], refs[29:31], refs[31]
    me = lax.axis_index("seq")
    i = pl.program_id(0)
    rows = k_ref.shape[0]
    step = HEADS_STEP * HEAD_WIDTH
    half = step // 2
    core = me % 2
    mate = me + 1 - 2 * core
    peers, has, ids = relations(me, count)
    order = peers[::-1]

    def chunk(j):
        return pl.ds(pl.multiple_of(j * step, HEAD_WIDTH), step)

    def edge(j, side, part, slot):
        ref = (k_ref, v_ref)[part]
        src = ref.at[pl.ds(side * (rows - BLK), BLK), chunk(j)]
        return remote(src, er.at[j, slot, part],
                      (edge_sems[0].at[j, side, part], edge_sems[1].at[j, slot, part]),
                      None, ids[side])

    def far(j, peer):
        k, n, r, dest, t, o = peer
        sems = (far_sems[0].at[j, n - 1 + r], far_sems[1].at[j, n - 1 + r])
        if n == 1:
            return remote(coarse[0].at[j], recv[0].at[j, 0], sems, None, dest)
        part = columns_of(t % 2, half)
        return remote(coarse[k].at[j, :, part], recv[k].at[j, o, :, part], sems, None, dest)

    def swap(j, peer, owner, side, sems):
        k, n, r = peer[:3]
        slot = recv[k].at[j, (owner % n + n - r) % n, :, columns_of(side, half)]
        return remote(slot, slot,
                      (sems[0].at[j, n - 1 + r], sems[1].at[j, n - 1 + r]), None, mate)

    def stores(j):
        pairs = [(l1.at[j], outs[0].at[:, :, chunk(j)])]
        pairs += [(recv[k].at[j], outs[1 + k].at[:, :, chunk(j)]) for k in range(len(FAR))]
        pairs.append((er.at[j], outs[5].at[:, :, :, chunk(j)]))
        return [pltpu.make_async_copy(src, dst, out_sem.at[j, n])
                for n, (src, dst) in enumerate(pairs)]

    def send(j, _):
        for part, ref in enumerate((k_ref, v_ref)):
            level = halve(ref[:, chunk(j)]).astype(BF16)
            l1[j, part] = level
            for scr, n in zip(coarse[:3], FAR):
                level = halve(level).astype(BF16)
                m = BLK // n
                scr[j, part * m:(part + 1) * m] = level
        coarse[3][j] = jnp.concatenate(
            [halve(coarse[2][j, :16]), halve(coarse[2][j, 16:])], 0).astype(BF16)
        for peer in order:
            far(j, peer).start()
        for side in range(2):
            @pl.when(has[side])
            def _():
                for part in range(2):
                    edge(j, side, part, 1 - side).start()
        return 0

    def receive(j):
        for peer in order:
            if peer[1] == 1:
                far(j, peer).wait_recv()
            else:
                swap(j, peer, me, core, far_sems).wait_recv()
                swap(j, peer, me, core, swap_sems).start()

    @pl.when(i == 0)
    def _():
        greet(peers, has, ids)
        lax.fori_loop(0, steps, send, 0)
        receive(0)

    for peer in order:
        if peer[1] > 1:
            swap(i, peer, mate, 1 - core, swap_sems).wait_recv()
    for side in range(2):
        @pl.when(has[side])
        def _():
            for part in range(2):
                edge(i, side, part, side).wait_recv()
    for copy in stores(i):
        copy.start()
    here = chunk(i)
    forward_kernel(count, q_ref, k_ref.at[:, here], v_ref.at[:, here], u_ref, gain_ref,
                   bias_ref, l1.at[i], *[ref.at[i] for ref in recv], er.at[i], *stats)

    @pl.when(i < steps - 1)
    def _():
        receive(i + 1)

    @pl.when(i == steps - 1)
    def _():
        def finish(j, _):
            for peer in order:
                far(j, peer).wait_send()
                if peer[1] > 1:
                    swap(j, peer, me, core, swap_sems).wait_send()
            for side in range(2):
                @pl.when(has[side])
                def _():
                    for part in range(2):
                        edge(j, side, part, 1 - side).wait_send()
            for copy in stores(j):
                copy.wait()
            return 0
        lax.fori_loop(0, steps, finish, 0)


def backward_kernel(count, q_ref, k_ref, v_ref, u_ref, gain_ref, bias_ref, l1_ref,
                    r2, r3, r4, r5, edge_ref, att_ref, lse_ref, coef_ref,
                    norm_ref, gq_ref, loc_ref, gl1_ref, g2, g3, g4, g5, eg_ref):
    me = lax.axis_index("seq")
    scale = HEAD_WIDTH ** -0.5
    for h in range(HEADS_STEP):
        c = slice(h * HEAD_WIDTH, (h + 1) * HEAD_WIDTH)
        keys, values = load_sets(me, count, c, k_ref, v_ref, l1_ref, (r2, r3, r4, r5), edge_ref)
        gain = gain_ref[:, c].astype(F32)
        terms = []
        for p in range(2):
            rows = slice(p * 2 * BLK, (p + 1) * 2 * BLK)
            q = q_ref[rows, c]
            inv, back = coef_ref[rows, 0:1], coef_ref[rows, 1:2]
            wide = att_ref[rows, c].astype(F32)
            sg = u_ref[rows, c].astype(F32) * gain
            norm_ref[rows, c] = (wide * inv * gain).astype(BF16)
            d = (inv * sg - wide * back).astype(BF16)
            s = dot(keys[p], q, NT) * (LOG2E * scale) + bias_ref[p]
            probs = jnp.exp2(s - lse_ref[h, :, rows])
            dp = dot(values[p], d, NT)
            inner = jnp.sum(probs * dp, 0, keepdims=True)
            ds = (probs * (dp - inner) * scale).astype(BF16)
            gq_ref[rows, c] = dot(ds, keys[p], TN).astype(BF16)
            terms.append((dot(ds, q, NN), dot(probs.astype(BF16), d, NN)))
        for part in range(2):
            a, b = terms[0][part], terms[1][part]
            eg_ref[0, part, :, c] = a[:BLK].astype(BF16)
            eg_ref[1, part, :, c] = b[3 * BLK:4 * BLK].astype(BF16)
            loc_ref[part, :, c] = jnp.concatenate(
                [a[BLK:2 * BLK], a[2 * BLK:4 * BLK] + b[:2 * BLK], b[2 * BLK:3 * BLK]], 0).astype(BF16)
            gl1_ref[part, :, c] = jnp.concatenate(
                [b[4 * BLK:5 * BLK], a[4 * BLK:5 * BLK]], 0).astype(BF16)
        both = [terms[0][part][5 * BLK:] + terms[1][part][5 * BLK:] for part in range(2)]
        for k, (n, g) in enumerate(zip(FAR, (g2, g3, g4, g5))):
            m = BLK // n
            parts = [x[k * BLK:(k + 1) * BLK].reshape(n, m, HEAD_WIDTH) for x in both]
            g[:, :, c] = jnp.concatenate(parts, 1).astype(BF16)


def derive_send_kernel(count, steps, *refs):
    ins, outs = refs[:15], refs[15:19]
    dst, er = refs[19:23], refs[23]
    g, eg, own, came = refs[24:28], refs[28], (None,) + refs[29:32], (None,) + refs[32:35]
    far_sems, swap_sems, edge_sems = refs[35:37], refs[37:39], refs[39:41]
    me = lax.axis_index("seq")
    i = pl.program_id(0)
    step = HEADS_STEP * HEAD_WIDTH
    half = step // 2
    core = me % 2
    mate = me + 1 - 2 * core
    peers, has, ids = relations(me, count)

    @pl.when(i == 0)
    def _():
        greet(peers, has, ids)

    backward_kernel(count, *ins, *outs, *[ref.at[i] for ref in g], eg.at[i])

    def chunk(j):
        return pl.ds(pl.multiple_of(j * step, HEAD_WIDTH), step)

    def edge(j, side, slot):
        return remote(eg.at[j, side], er.at[slot, :, :, chunk(j)],
                      (edge_sems[0].at[j, side], edge_sems[1].at[j, slot]), None, ids[side])

    def swap(j, k):
        return remote(g[k].at[j, :, :, columns_of(1 - core, half)], came[k].at[j],
                      (swap_sems[0].at[j, k], swap_sems[1].at[j, k]), None, mate)

    def far(j, peer):
        k, n, r, dest, t, o = peer
        sems = (far_sems[0].at[j, n - 1 + r], far_sems[1].at[j, n - 1 + r])
        if k == 0:
            return remote(g[0].at[j, t], dst[0].at[o, :, chunk(j)], sems, None, dest)
        place = pl.ds(pl.multiple_of(j * step + core * half, HEAD_WIDTH), half)
        return remote(own[k].at[j, t], dst[k].at[o // 2, :, place], sems, None, dest)

    for k in (3, 2, 1):
        swap(i, k).start()
    for side in range(2):
        @pl.when(has[side])
        def _():
            edge(i, side, 1 - side).start()
    far(i, peers[0]).start()

    def send_sums(j):
        for level in (3, 2, 1):
            swap(j, level).wait()
            mine = g[level][j, :, :, columns_of(core, half)].astype(F32)
            own[level][j] = (mine + came[level][j].astype(F32)).astype(BF16)
            for peer in peers:
                if peer[0] == level:
                    far(j, peer).start()

    @pl.when(i > 0)
    def _():
        send_sums(i - 1)

    @pl.when(i == steps - 1)
    def _():
        send_sums(i)

        def finish(j, _):
            for peer in peers:
                far(j, peer).wait()
            for side in range(2):
                @pl.when(has[side])
                def _():
                    edge(j, side, 1 - side).wait_send()
                    edge(j, side, side).wait_recv()
            return 0
        lax.fori_loop(0, steps, finish, 0)


def combine_kernel(count, loc_ref, gl1_ref, r2, r3, r4, r5, er_ref, gk_ref, gv_ref):
    me = lax.axis_index("seq")
    row_count, span = gk_ref.shape
    flags = (me > 0, me < count - 1)
    sizes = [ref.shape[0] * ref.shape[1] // 2 for ref in (r2, r3, r4, r5)]
    width = 2 * BLK + sum(sizes)
    row = lax.broadcasted_iota(jnp.int32, (row_count, width), 0)
    col = lax.broadcasted_iota(jnp.int32, (row_count, width), 1)
    mat = jnp.where((col < 2 * BLK) & (row // 2 == col), 0.5, 0.0)
    for k, n in enumerate(FAR):
        first = 2 * BLK + sum(sizes[:k])
        m = BLK // n
        inside = (col >= first) & (col < first + sizes[k])
        mat += jnp.where(inside & (row // (4 * n) == (col - first) % m), 0.25 / n, 0.0)
    mat = mat.astype(BF16)
    for part, out in enumerate((gk_ref, gv_ref)):
        far = [gl1_ref[part]]
        for n, ref in zip(FAR, (r2, r3, r4, r5)):
            m = BLK // n
            if m >= 16:
                far.append(ref[:, part * m:(part + 1) * m, :].reshape(-1, span))
            else:
                wide = ref[...].astype(F32)
                far.append(wide[:, part * m:(part + 1) * m].reshape(-1, span).astype(BF16))
        total = loc_ref[part].astype(F32) + dot(mat, jnp.concatenate(far, 0), NN)
        low = jnp.where(flags[0], er_ref[0, part].astype(F32), 0.0)
        high = jnp.where(flags[1], er_ref[1, part].astype(F32), 0.0)
        out[:BLK] = (total[:BLK] + low).astype(BF16)
        out[BLK:row_count - BLK] = total[BLK:row_count - BLK].astype(BF16)
        out[row_count - BLK:] = (total[row_count - BLK:] + high).astype(BF16)


def score_bias(seq_index, seq_count):
    key = jnp.arange(4 * BLK)[None, :, None] // BLK
    query = jnp.arange(2 * BLK)[None, None, :] // BLK
    pair = jnp.arange(2)[:, None, None]
    block = seq_index * 4 + 2 * pair + key - 1
    valid = (key >= query) & (key <= query + 2) & (block >= 0) & (block < 4 * seq_count)
    band = jnp.where(valid, 0.0, -1e30).astype(F32)
    levels = jnp.repeat(jnp.arange(1, LEV + 1).astype(F32), BLK)[None, :, None]
    return jnp.concatenate([band, jnp.broadcast_to(levels, (2, LEV * BLK, 2 * BLK))], 1)


def body(queries, keys_in, values_in, gain, upstream):
    rows, cols = queries.shape
    heads = cols // HEAD_WIDTH
    me = lax.axis_index("seq")
    count = lax.axis_size("seq")
    shape = jax.ShapeDtypeStruct
    any_spec = pl.BlockSpec(memory_space=pl.ANY)
    vmem = pl.BlockSpec(memory_space=pltpu.VMEM)
    pieces = piece_shapes(cols)
    piece_out = [shape(s, BF16) for s in pieces]
    edge_out = shape((2, 2, BLK, cols), BF16)
    limit = 48 * 1024 * 1024

    bias = score_bias(me, count)
    gain2 = gain.reshape(1, cols)

    step = HEADS_STEP * HEAD_WIDTH
    grid = (heads // HEADS_STEP,)
    flat = lambda n: pl.BlockSpec((n, step), lambda i: (0, i))
    cube = lambda a, b: pl.BlockSpec((a, b, step), lambda i: (0, 0, i))
    quad = pl.BlockSpec((2, 2, BLK, step), lambda i: (0, 0, 0, i))
    fixed = lambda s: pl.BlockSpec(s, lambda i: (0,) * len(s))
    piece_specs = [cube(s[0], s[1]) for s in pieces]
    lse_spec = pl.BlockSpec((HEADS_STEP, 1, rows), lambda i: (i, 0, 0))
    shared = [flat(rows)] * 4 + [flat(1), fixed(bias.shape), cube(2, rows // 2)] + piece_specs + [quad]
    params = pltpu.CompilerParams(vmem_limit_bytes=limit)
    steps = grid[0]
    dma = pltpu.SemaphoreType.DMA
    chunks = [pltpu.VMEM((steps,) + s[:2] + (step,), BF16) for s in pieces]
    edges = pltpu.VMEM((steps, 2, 2, BLK, step), BF16)
    att, lse, stat, l1, *recv = pl.pallas_call(
        functools.partial(gather_attend_kernel, count, steps),
        grid=grid,
        out_shape=[shape((rows, cols), BF16), shape((heads, 1, rows), F32),
                   shape((2, rows, HEAD_WIDTH), F32), shape((2, rows // 2, cols), BF16)]
        + piece_out + [edge_out],
        in_specs=[flat(rows), vmem, vmem, flat(rows), flat(1), fixed(bias.shape)],
        out_specs=[flat(rows), lse_spec, fixed((2, rows, HEAD_WIDTH))] + [any_spec] * 6,
        scratch_shapes=[pltpu.VMEM((steps, 2, rows // 2, step), BF16)] + chunks + [edges]
        + [pltpu.VMEM((steps, s[1], step), BF16) for s in pieces]
        + [dma((steps, sum(FAR)))] * 4 + [dma((steps, 2, 2))] * 2 + [dma((steps, 6))],
        compiler_params=pltpu.CompilerParams(
            collective_id=0, has_side_effects=True, vmem_limit_bytes=limit),
        name="gather_and_attend",
    )(queries, keys_in, values_in, upstream, gain2, bias)
    common = (queries, keys_in, values_in, upstream, gain2, bias, l1, *recv)

    sums = jnp.sum(stat, -1)
    parts = lax.axis_size("head")
    total = sums
    for shift in range(1, parts):
        total = total + lax.ppermute(
            sums, "head", [(i, (i + shift) % parts) for i in range(parts)])
    columns = cols * parts
    inv = lax.rsqrt(total[0] / columns + EPSILON)
    coef = jnp.stack([inv, inv * inv * inv * total[1] / columns], 1)

    summed = [(max(1, s[0] // 2),) + s[1:] for s in pieces]
    halves = [pltpu.VMEM((steps,) + s[:2] + (step // 2,), BF16) for s in pieces[1:]]
    normed, gq, loc, gl1, *back = pl.pallas_call(
        functools.partial(derive_send_kernel, count, steps),
        grid=grid,
        out_shape=[shape((rows, cols), BF16)] * 2
        + [shape((2, rows, cols), BF16), shape((2, rows // 2, cols), BF16)]
        + [shape(s, BF16) for s in summed] + [edge_out],
        in_specs=shared + [flat(rows), lse_spec, fixed((rows, 2))],
        out_specs=[flat(rows)] * 2 + [cube(2, rows), cube(2, rows // 2)] + [any_spec] * 5,
        scratch_shapes=chunks + [edges] + halves * 2
        + [dma((steps, sum(FAR)))] * 2 + [dma((steps, LEV - 1))] * 2 + [dma((steps, 2))] * 2,
        compiler_params=pltpu.CompilerParams(
            collective_id=1, has_side_effects=True, vmem_limit_bytes=limit),
        name="differentiate_and_send",
    )(*common, att, lse, coef)

    gk, gv = pl.pallas_call(
        functools.partial(combine_kernel, count),
        grid=grid,
        out_shape=[shape((rows, cols), BF16)] * 2,
        in_specs=[cube(2, rows), cube(2, rows // 2)]
        + [cube(s[0], s[1]) for s in summed] + [quad],
        out_specs=[flat(rows)] * 2,
        compiler_params=params,
        name="combine",
    )(loc, gl1, *back)
    return normed, gq, gk, gv


def solution(mesh):
    spec = P("seq", "head")
    return jax.shard_map(
        body,
        mesh=mesh,
        in_specs=(spec, spec, spec, P("head"), spec),
        out_specs=(spec,) * 4,
        check_vma=False,
    )
```
